512 devices in a mesh: fsdp: 128 (over y, z, core), rep: 4 (over x).
Axes of the slice: x: 4, y: 8, z: 8, core: 2. Of those that a mesh axis runs over, the one named last changes fastest.
Arguments:
- grads: bfloat16 [128, 1024, 1024], P(None, 'fsdp'), may hold values from -96 to 96
- owners: int32 [128], replicated, may hold values from 0 to 127, as said below
- counts: int32 [128], replicated, may hold values from 0 to 2, as said below
Outputs:
- preconditioned: bfloat16 [128, 1024, 1024], P(None, 'fsdp')
The draws below stay inside these ranges and needn't reach their ends.
Inputs may be any that keep to these rules, and one draw needn't show every extreme that they name: `owners`: no owner is named by more than 2 entries, and some owner by exactly 2. counts[o] is the number of entries of owners equal to o, or one less; some owner named by 2 entries has counts equal to 2.
All inputs are finite; a program needn't handle non-finite values.
Results may differ from the reference program's by a relative error of at most 0.0068.
Values may be sent and summed in bfloat16 or wider, within the bound.
No kernel may reach another device: no remote copies, remote signals or barrier semaphores. Data moves between devices by JAX's collectives and lax.ppermute only.
A program may use at most 64 MiB of HBM per device.

```python
import jax
import jax.numpy as jnp
from jax import lax

B = 1024
CAP = 2
NB = 128
N_FSDP = 128


def assign_owners(key):
    total = N_FSDP * CAP
    base = jax.random.permutation(jax.random.fold_in(key, 11), total)
    lucky = jax.random.randint(jax.random.fold_in(key, 12), (), 0, N_FSDP)
    places = jnp.arange(total, dtype=jnp.int32)
    score = jnp.where(places // CAP == lucky, -2, base)
    score = jnp.where(places == (N_FSDP - 1) * CAP, jnp.minimum(score, -1), score)
    order = jnp.argsort(score, stable=True)
    chosen = order[:NB] // CAP
    shuffle = jax.random.permutation(jax.random.fold_in(key, 13), NB)
    return (chosen[shuffle].astype(jnp.int32), lucky)


def row_scaled(key, top, side, entries):
    rows = jnp.arange(B, dtype=jnp.float32) / (B - 1)
    scale = jnp.exp(jnp.log(top) * rows)
    cols = jnp.exp(jnp.log(side) * rows)
    return entries * scale[None, :, None] * cols[None, None, :]


def draw_grads(key, part):
    key = jax.random.fold_in(key, 3)
    entries = jax.random.truncated_normal(key, -6.0, 6.0, (NB, B, B), jnp.float32)
    return row_scaled(key, 4.0, 4.0, entries).astype(jnp.bfloat16)


def draw_owners(key, part):
    owners, lucky = assign_owners(key)
    return owners


def draw_counts(key, part):
    owners, lucky = assign_owners(key)
    key = jax.random.fold_in(key, 2)
    match = owners[None, :] == jnp.arange(N_FSDP, dtype=jnp.int32)[:, None]
    present = jnp.sum(match.astype(jnp.int32), axis=1)
    dropped = jax.random.randint(key, (N_FSDP,), 0, 2).astype(jnp.int32)
    dropped = jnp.where(jnp.arange(N_FSDP, dtype=jnp.int32) == lucky, 0, dropped)
    return jnp.maximum(present - dropped, 0).astype(jnp.int32)


def setup_inputs(seed: int = 0) -> dict:
    streams_of = jax.random.split(jax.random.key(seed), 4)
    grads = draw_grads(jax.random.fold_in(streams_of[3], 71), 0)
    owners = draw_owners(jax.random.fold_in(streams_of[3], 71), 0)
    counts = draw_counts(jax.random.fold_in(streams_of[3], 71), 0)
    return dict(grads=grads, owners=owners, counts=counts)


EPS = 1e-06

def refresh_one(block):
    wide = block.astype(jnp.float32)
    total_sq = jnp.sum(wide * wide)
    scale_c = total_sq / B + EPS
    root = scale_c ** (-0.25)
    ident = jnp.eye(B, dtype=jnp.float32)
    left = jnp.dot(block, block.T, preferred_element_type=jnp.float32)
    right = jnp.dot(block.T, block, preferred_element_type=jnp.float32)
    x_left = (root * (5.0 * ident - (left + EPS * ident) / scale_c) / 4.0).astype(jnp.bfloat16)
    x_right = (root * (5.0 * ident - (right + EPS * ident) / scale_c) / 4.0).astype(jnp.bfloat16)
    hidden = jnp.dot(x_left, block, preferred_element_type=jnp.float32).astype(jnp.bfloat16)
    product = jnp.dot(hidden, x_right, preferred_element_type=jnp.float32)
    graft = jnp.sqrt((total_sq + EPS) / (jnp.sum(product * product) + EPS))
    return (product * graft).astype(jnp.bfloat16)

def reference(grads, owners, counts):
    blocks = owners.shape[0]
    index = jnp.arange(blocks, dtype=jnp.int32)
    same = owners[:, None] == owners[None, :]
    earlier = index[None, :] < index[:, None]
    slot = lax.optimization_barrier(jnp.sum((same & earlier).astype(jnp.int32), axis=1))
    groups = counts.shape[0]
    have = lax.optimization_barrier(jnp.sum(jnp.where(owners[:, None] == jnp.arange(groups, dtype=jnp.int32)[None, :], counts[None, :], 0), axis=1))
    valid = slot < have
    result = lax.map(refresh_one, grads)
    return jnp.where(valid[:, None, None], result, jnp.zeros_like(result))
```

```python
import jax
import jax.numpy as jnp
from jax import lax
from jax.experimental import pallas as pl
from jax.experimental.pallas import tpu as pltpu
from jax.sharding import Mesh
from jax.sharding import PartitionSpec as P

EPS = 1e-06
TILE = 256


def first_dims(a, b):
    return lax.dot_general(a, b, (((0,), (0,)), ((), ())), preferred_element_type=jnp.float32)


def refresh_kernel(block_ref, owners_ref, counts_ref, mine_ref, theirs_ref, out_ref, right, root_r, product):
    rows, width = mine_ref.shape
    places = lax.broadcasted_iota(jnp.int32, owners_ref.shape, 1)
    block = block_ref[0]
    owners = owners_ref[...]
    owner = jnp.sum(jnp.where(places == block, owners, 0))
    slot = jnp.sum(jnp.where((owners == owner) & (places < block), 1, 0))
    have = jnp.sum(jnp.where(places == owner, counts_ref[...], 0))
    valid = (slot < have).astype(jnp.float32)

    total_sq = jnp.zeros((1, 1), jnp.float32)
    for j in range(0, width, TILE):
        cols = pl.ds(j, TILE)
        tile = first_dims(mine_ref[...], mine_ref[:, cols]) + first_dims(theirs_ref[...], theirs_ref[:, cols])
        right[:, cols] = tile
        diag = right[cols, cols]
        r = lax.broadcasted_iota(jnp.int32, diag.shape, 0)
        c = lax.broadcasted_iota(jnp.int32, diag.shape, 1)
        total_sq += jnp.sum(jnp.where(r == c, diag, 0.0), keepdims=True)

    scale_c = total_sq / width + EPS
    quarter = lax.rsqrt(jnp.sqrt(scale_c)) * 0.25
    slope = quarter / scale_c
    for j in range(0, width, TILE):
        cols = pl.ds(j, TILE)
        tile = right[:, cols]
        r = lax.broadcasted_iota(jnp.int32, tile.shape, 0)
        c = lax.broadcasted_iota(jnp.int32, tile.shape, 1) + j
        diag = 5.0 * quarter - EPS * slope
        root_r[:, cols] = (jnp.where(r == c, diag, 0.0) - slope * tile).astype(jnp.bfloat16)

    product_sq = jnp.zeros((1, 1), jnp.float32)
    for ref, keep in ((mine_ref, True), (theirs_ref, False)):
        for i in range(0, rows, TILE):
            part = pl.ds(i, TILE)
            hidden = jnp.dot(ref[part, :], root_r[...], preferred_element_type=jnp.float32)
            done = jnp.dot(hidden.astype(jnp.bfloat16), root_r[...], preferred_element_type=jnp.float32)
            product_sq += jnp.sum(done * done, keepdims=True)
            if keep:
                product[part, :] = done
    graft = jnp.sqrt((total_sq + EPS) / (product_sq + EPS)) * valid
    out_ref[...] = (product[...] * graft).astype(jnp.bfloat16)


def refresh(block, owners, counts, mine, theirs):
    rows, width = mine.shape
    vmem = pl.BlockSpec(memory_space=pltpu.VMEM)
    return pl.pallas_call(
        refresh_kernel,
        out_shape=jax.ShapeDtypeStruct((rows, width), jnp.bfloat16),
        in_specs=[pl.BlockSpec(memory_space=pltpu.SMEM), vmem, vmem, vmem, vmem],
        out_specs=vmem,
        scratch_shapes=[
            pltpu.VMEM((width, width), jnp.float32),
            pltpu.VMEM((width, width), jnp.bfloat16),
            pltpu.VMEM((rows, width), jnp.float32),
        ],
        compiler_params=pltpu.CompilerParams(vmem_limit_bytes=40 * 2**20),
        cost_estimate=pl.CostEstimate(flops=6 * width**3, bytes_accessed=6 * rows * width, transcendentals=0),
    )(block, owners, counts, mine, theirs)


def body(grads, owners, counts):
    blocks, rows_dev, width = grads.shape
    chips = lax.axis_size("yz")
    planes = lax.axis_size("x")
    half = chips // 2
    side = lax.axis_index("x") % 2
    block = side * chips + lax.axis_index("yz")

    outgoing = lax.dynamic_slice_in_dim(grads, side * chips, chips, 0)
    mine = lax.all_to_all(outgoing, "yz", split_axis=0, concat_axis=0, tiled=True)
    mine = mine.reshape(chips * rows_dev, width)
    theirs = lax.ppermute(mine, "c", [(0, 1), (1, 0)])
    done = refresh(
        block.astype(jnp.int32).reshape(1), owners.reshape(1, -1), counts.reshape(1, -1), mine, theirs
    )
    back = lax.all_to_all(
        done.reshape(chips, rows_dev, width), "yz", split_axis=0, concat_axis=0, tiled=True
    )
    up = [(i, (i + 1) % planes) for i in range(planes)]
    down = [(i, (i - 1) % planes) for i in range(planes)]
    low = lax.ppermute(back[:half], "x", up)
    high = lax.ppermute(back[half:], "x", down)
    result = jnp.zeros((blocks, rows_dev, width), jnp.bfloat16)
    result = lax.dynamic_update_slice_in_dim(result, back, side * chips, 0)
    result = lax.dynamic_update_slice_in_dim(result, low, (1 - side) * chips, 0)
    return lax.dynamic_update_slice_in_dim(result, high, (1 - side) * chips + half, 0)


def solution(mesh):
    fine = Mesh(mesh.devices.reshape(64, 2, 4), ("yz", "c", "x"))
    rows = P(None, ("yz", "c"), None)
    return jax.shard_map(body, mesh=fine, in_specs=(rows, P(), P()), out_specs=rows, check_vma=False)
```

```python
import jax
import jax.numpy as jnp
from jax import lax
from jax.experimental import pallas as pl
from jax.experimental.pallas import tpu as pltpu
from jax.sharding import Mesh
from jax.sharding import PartitionSpec as P

EPS = 1e-06
TILE = 256


def first_dims(a, b):
    return lax.dot_general(a, b, (((0,), (0,)), ((), ())), preferred_element_type=jnp.float32)


def gram_kernel(rows_ref, out_ref):
    width = rows_ref.shape[1]
    for j in range(0, width, TILE):
        out_ref[j:, j : j + TILE] = first_dims(rows_ref[:, j:], rows_ref[:, j : j + TILE])


def gram(rows):
    count, width = rows.shape
    vmem = pl.BlockSpec(memory_space=pltpu.VMEM)
    return pl.pallas_call(
        gram_kernel,
        out_shape=jax.ShapeDtypeStruct((width, width), jnp.float32),
        in_specs=[vmem],
        out_specs=vmem,
        compiler_params=pltpu.CompilerParams(vmem_limit_bytes=24 * 2**20),
        cost_estimate=pl.CostEstimate(
            flops=2 * count * width**2, bytes_accessed=2 * count * width + 4 * width**2, transcendentals=0
        ),
    )(rows)


def on_diagonal(tile):
    r = lax.broadcasted_iota(jnp.int32, tile.shape, 0)
    c = lax.broadcasted_iota(jnp.int32, tile.shape, 1)
    return r == c


def refresh_kernel(
    block_ref, owners_ref, counts_ref, mine_ref, theirs_ref, gram_ref, out_ref, right, root_r, rest, product
):
    rows, width = mine_ref.shape
    places = lax.broadcasted_iota(jnp.int32, owners_ref.shape, 1)
    block = block_ref[0]
    owners = owners_ref[...]
    owner = jnp.sum(jnp.where(places == block, owners, 0))
    slot = jnp.sum(jnp.where((owners == owner) & (places < block), 1, 0))
    have = jnp.sum(jnp.where(places == owner, counts_ref[...], 0))
    valid = (slot < have).astype(jnp.float32)

    total_sq = jnp.zeros((1, 1), jnp.float32)
    for j in range(0, width, TILE):
        tile = gram_ref[j:, j : j + TILE] + first_dims(theirs_ref[:, j:], theirs_ref[:, j : j + TILE])
        right[j:, j : j + TILE] = tile
        top = tile[:TILE, :]
        total_sq += jnp.sum(jnp.where(on_diagonal(top), top, 0.0), keepdims=True)

    scale_c = total_sq / width + EPS
    quarter = lax.rsqrt(jnp.sqrt(scale_c)) * 0.25
    slope = quarter / scale_c
    diag = 5.0 * quarter - EPS * slope
    for j in range(0, width, TILE):
        cols = slice(j, j + TILE)
        tile = -slope * right[cols, cols]
        tile = jnp.where(on_diagonal(tile), diag + tile, tile)
        kept = tile.astype(jnp.bfloat16)
        root_r[cols, cols] = kept
        off = jnp.where(on_diagonal(tile), tile - kept.astype(jnp.float32), 0.0)
        rest[:, cols] = 2.0 * jnp.sum(off, axis=0, keepdims=True)
        if j + TILE < width:
            below = (-slope * right[j + TILE :, cols]).astype(jnp.bfloat16)
            root_r[j + TILE :, cols] = below
            root_r[cols, j + TILE :] = below.T

    product_sq = jnp.zeros((1, 1), jnp.float32)
    for ref, keep in ((mine_ref, True), (theirs_ref, False)):
        for i in range(0, rows, TILE):
            hidden = jnp.dot(ref[i : i + TILE, :], root_r[...], preferred_element_type=jnp.float32)
            done = jnp.dot(hidden.astype(jnp.bfloat16), root_r[...], preferred_element_type=jnp.float32)
            done = done + hidden * rest[...]
            product_sq += jnp.sum(done * done, keepdims=True)
            if keep:
                product[i : i + TILE, :] = done
    graft = jnp.sqrt((total_sq + EPS) / (product_sq + EPS)) * valid
    out_ref[...] = (product[...] * graft).astype(jnp.bfloat16)


def refresh(block, owners, counts, mine, theirs, mine_gram):
    rows, width = mine.shape
    vmem = pl.BlockSpec(memory_space=pltpu.VMEM)
    return pl.pallas_call(
        refresh_kernel,
        out_shape=jax.ShapeDtypeStruct((rows, width), jnp.bfloat16),
        in_specs=[pl.BlockSpec(memory_space=pltpu.SMEM), vmem, vmem, vmem, vmem, vmem],
        out_specs=vmem,
        scratch_shapes=[
            pltpu.VMEM((width, width), jnp.float32),
            pltpu.VMEM((width, width), jnp.bfloat16),
            pltpu.VMEM((1, width), jnp.float32),
            pltpu.VMEM((rows, width), jnp.float32),
        ],
        compiler_params=pltpu.CompilerParams(vmem_limit_bytes=40 * 2**20),
        cost_estimate=pl.CostEstimate(flops=5 * width**3, bytes_accessed=6 * rows * width, transcendentals=0),
    )(block, owners, counts, mine, theirs, mine_gram)


def place_own_kernel(side_ref, own_ref, out_ref, sem):
    half = own_ref.shape[0]
    copy = pltpu.make_async_copy(own_ref, out_ref.at[pl.ds(side_ref[0] * half, half)], sem)
    copy.start()
    copy.wait()


def place_own(side, own, blocks):
    any_space = pl.BlockSpec(memory_space=pl.ANY)
    return pl.pallas_call(
        place_own_kernel,
        out_shape=jax.ShapeDtypeStruct((blocks,) + own.shape[1:], own.dtype),
        in_specs=[pl.BlockSpec(memory_space=pltpu.SMEM), any_space],
        out_specs=pl.BlockSpec(memory_space=pltpu.HBM),
        scratch_shapes=[pltpu.SemaphoreType.DMA],
        cost_estimate=pl.CostEstimate(flops=0, bytes_accessed=4 * own.size, transcendentals=0),
    )(side, own)


def place_others_kernel(side_ref, held_ref, low_ref, high_ref, out_ref, low_sem, high_sem):
    part = low_ref.shape[0]
    start = (1 - side_ref[0]) * (2 * part)
    low = pltpu.make_async_copy(low_ref, out_ref.at[pl.ds(start, part)], low_sem)
    high = pltpu.make_async_copy(high_ref, out_ref.at[pl.ds(start + part, part)], high_sem)
    low.start()
    high.start()
    low.wait()
    high.wait()


def place_others(side, held, low, high):
    any_space = pl.BlockSpec(memory_space=pl.ANY)
    hbm = pl.BlockSpec(memory_space=pltpu.HBM)
    return pl.pallas_call(
        place_others_kernel,
        out_shape=jax.ShapeDtypeStruct(held.shape, held.dtype),
        in_specs=[pl.BlockSpec(memory_space=pltpu.SMEM), hbm, any_space, any_space],
        out_specs=hbm,
        scratch_shapes=[pltpu.SemaphoreType.DMA, pltpu.SemaphoreType.DMA],
        input_output_aliases={1: 0},
        cost_estimate=pl.CostEstimate(flops=0, bytes_accessed=8 * low.size, transcendentals=0),
    )(side, held, low, high)


def body(grads, owners, counts):
    blocks, rows_dev, width = grads.shape
    chips = lax.axis_size("yz")
    planes = lax.axis_size("x")
    half = chips // 2
    side = (lax.axis_index("x") % 2).astype(jnp.int32)
    block = side * chips + lax.axis_index("yz").astype(jnp.int32)
    side_ref = side.reshape(1)

    outgoing = lax.dynamic_slice_in_dim(grads, side * chips, chips, 0)
    mine = lax.all_to_all(outgoing, "yz", split_axis=0, concat_axis=0, tiled=True)
    mine = mine.reshape(chips * rows_dev, width)
    theirs = lax.ppermute(mine, "c", [(0, 1), (1, 0)])
    done = refresh(
        block.reshape(1), owners.reshape(1, -1), counts.reshape(1, -1), mine, theirs, gram(mine)
    )
    back = lax.all_to_all(
        done.reshape(chips, rows_dev, width), "yz", split_axis=0, concat_axis=0, tiled=True
    )
    up = [(i, (i + 1) % planes) for i in range(planes)]
    down = [(i, (i - 1) % planes) for i in range(planes)]
    low = lax.ppermute(back[:half], "x", up)
    high = lax.ppermute(back[half:], "x", down)
    held = place_own(side_ref, back, blocks)
    return place_others(side_ref, held, low, high)


def solution(mesh):
    fine = Mesh(mesh.devices.reshape(64, 2, 4), ("yz", "c", "x"))
    rows = P(None, ("yz", "c"), None)
    return jax.shard_map(body, mesh=fine, in_specs=(rows, P(), P()), out_specs=rows, check_vma=False)
```

```python
import jax
import jax.numpy as jnp
from jax import lax
from jax.experimental import pallas as pl
from jax.experimental.pallas import tpu as pltpu
from jax.sharding import Mesh
from jax.sharding import PartitionSpec as P

EPS = 1e-06
TILE = 256


def first_dims(a, b):
    return lax.dot_general(a, b, (((0,), (0,)), ((), ())), preferred_element_type=jnp.float32)


def gram_kernel(rows_ref, out_ref):
    width = rows_ref.shape[1]
    for j in range(0, width, TILE):
        out_ref[j:, j : j + TILE] = first_dims(rows_ref[:, j:], rows_ref[:, j : j + TILE])


def gram(rows):
    count, width = rows.shape
    vmem = pl.BlockSpec(memory_space=pltpu.VMEM)
    return pl.pallas_call(
        gram_kernel,
        out_shape=jax.ShapeDtypeStruct((width, width), jnp.float32),
        in_specs=[vmem],
        out_specs=vmem,
        compiler_params=pltpu.CompilerParams(vmem_limit_bytes=24 * 2**20),
        cost_estimate=pl.CostEstimate(
            flops=2 * count * width**2, bytes_accessed=2 * count * width + 4 * width**2, transcendentals=0
        ),
    )(rows)


def on_diagonal(tile):
    r = lax.broadcasted_iota(jnp.int32, tile.shape, 0)
    c = lax.broadcasted_iota(jnp.int32, tile.shape, 1)
    return r == c


def refresh_kernel(
    block_ref, owners_ref, counts_ref, mine_ref, theirs_ref, gram_ref, out_ref, right, root_r, rest, product
):
    rows, width = mine_ref.shape
    places = lax.broadcasted_iota(jnp.int32, owners_ref.shape, 1)
    block = block_ref[0]
    owners = owners_ref[...]
    owner = jnp.sum(jnp.where(places == block, owners, 0))
    slot = jnp.sum(jnp.where((owners == owner) & (places < block), 1, 0))
    have = jnp.sum(jnp.where(places == owner, counts_ref[...], 0))
    valid = (slot < have).astype(jnp.float32)

    total_sq = jnp.zeros((1, 1), jnp.float32)
    for j in range(0, width, TILE):
        tile = gram_ref[j:, j : j + TILE] + first_dims(theirs_ref[:, j:], theirs_ref[:, j : j + TILE])
        right[j:, j : j + TILE] = tile
        top = tile[:TILE, :]
        total_sq += jnp.sum(jnp.where(on_diagonal(top), top, 0.0), keepdims=True)

    scale_c = total_sq / width + EPS
    quarter = lax.rsqrt(jnp.sqrt(scale_c)) * 0.25
    slope = quarter / scale_c
    diag = 5.0 * quarter - EPS * slope
    for j in range(0, width, TILE):
        cols = slice(j, j + TILE)
        tile = -slope * right[cols, cols]
        tile = jnp.where(on_diagonal(tile), diag + tile, tile)
        kept = tile.astype(jnp.bfloat16)
        root_r[cols, cols] = kept
        off = jnp.where(on_diagonal(tile), tile - kept.astype(jnp.float32), 0.0)
        rest[:, cols] = 2.0 * jnp.sum(off, axis=0, keepdims=True)
        if j + TILE < width:
            below = (-slope * right[j + TILE :, cols]).astype(jnp.bfloat16)
            root_r[j + TILE :, cols] = below
            root_r[cols, j + TILE :] = below.T

    product_sq = jnp.zeros((1, 1), jnp.float32)
    for ref, keep in ((mine_ref, True), (theirs_ref, False)):
        for i in range(0, rows, TILE):
            hidden = jnp.dot(ref[i : i + TILE, :], root_r[...], preferred_element_type=jnp.float32)
            done = jnp.dot(hidden.astype(jnp.bfloat16), root_r[...], preferred_element_type=jnp.float32)
            done = done + hidden * rest[...]
            product_sq += jnp.sum(done * done, keepdims=True)
            if keep:
                product[i : i + TILE, :] = done
    graft = jnp.sqrt((total_sq + EPS) / (product_sq + EPS)) * valid
    out_ref[...] = (product[...] * graft).astype(jnp.bfloat16)


def refresh(block, owners, counts, mine, theirs, mine_gram):
    rows, width = mine.shape
    vmem = pl.BlockSpec(memory_space=pltpu.VMEM)
    return pl.pallas_call(
        refresh_kernel,
        out_shape=jax.ShapeDtypeStruct((rows, width), jnp.bfloat16),
        in_specs=[pl.BlockSpec(memory_space=pltpu.SMEM), vmem, vmem, vmem, vmem, vmem],
        out_specs=vmem,
        scratch_shapes=[
            pltpu.VMEM((width, width), jnp.float32),
            pltpu.VMEM((width, width), jnp.bfloat16),
            pltpu.VMEM((1, width), jnp.float32),
            pltpu.VMEM((rows, width), jnp.float32),
        ],
        compiler_params=pltpu.CompilerParams(vmem_limit_bytes=40 * 2**20),
        cost_estimate=pl.CostEstimate(flops=5 * width**3, bytes_accessed=6 * rows * width, transcendentals=0),
    )(block, owners, counts, mine, theirs, mine_gram)


def place_own_kernel(side_ref, own_ref, out_ref, sem):
    half = own_ref.shape[0]
    copy = pltpu.make_async_copy(own_ref, out_ref.at[pl.ds(side_ref[0] * half, half)], sem)
    copy.start()
    copy.wait()


def place_own(side, own, blocks):
    vmem = pl.BlockSpec(memory_space=pltpu.VMEM)
    return pl.pallas_call(
        place_own_kernel,
        out_shape=jax.ShapeDtypeStruct((blocks,) + own.shape[1:], own.dtype),
        in_specs=[pl.BlockSpec(memory_space=pltpu.SMEM), vmem],
        out_specs=pl.BlockSpec(memory_space=pltpu.HBM),
        scratch_shapes=[pltpu.SemaphoreType.DMA],
        cost_estimate=pl.CostEstimate(flops=0, bytes_accessed=4 * own.size, transcendentals=0),
    )(side, own)


def place_others_kernel(side_ref, held_ref, low_ref, high_ref, out_ref, low_sem, high_sem):
    part = low_ref.shape[0]
    start = (1 - side_ref[0]) * (2 * part)
    low = pltpu.make_async_copy(low_ref, out_ref.at[pl.ds(start, part)], low_sem)
    high = pltpu.make_async_copy(high_ref, out_ref.at[pl.ds(start + part, part)], high_sem)
    low.start()
    high.start()
    low.wait()
    high.wait()


def place_others(side, held, low, high):
    vmem = pl.BlockSpec(memory_space=pltpu.VMEM)
    hbm = pl.BlockSpec(memory_space=pltpu.HBM)
    return pl.pallas_call(
        place_others_kernel,
        out_shape=jax.ShapeDtypeStruct(held.shape, held.dtype),
        in_specs=[pl.BlockSpec(memory_space=pltpu.SMEM), hbm, vmem, vmem],
        out_specs=hbm,
        scratch_shapes=[pltpu.SemaphoreType.DMA, pltpu.SemaphoreType.DMA],
        input_output_aliases={1: 0},
        cost_estimate=pl.CostEstimate(flops=0, bytes_accessed=8 * low.size, transcendentals=0),
    )(side, held, low, high)


def body(grads, owners, counts):
    blocks, rows_dev, width = grads.shape
    chips = lax.axis_size("yz")
    planes = lax.axis_size("x")
    half = chips // 2
    side = (lax.axis_index("x") % 2).astype(jnp.int32)
    block = side * chips + lax.axis_index("yz").astype(jnp.int32)
    side_ref = side.reshape(1)

    outgoing = lax.dynamic_slice_in_dim(grads, side * chips, chips, 0)
    mine = lax.all_to_all(outgoing, "yz", split_axis=0, concat_axis=0, tiled=True)
    mine = mine.reshape(chips * rows_dev, width)
    theirs = lax.ppermute(mine, "c", [(0, 1), (1, 0)])
    done = refresh(
        block.reshape(1), owners.reshape(1, -1), counts.reshape(1, -1), mine, theirs, gram(mine)
    )
    back = lax.all_to_all(
        done.reshape(chips, rows_dev, width), "yz", split_axis=0, concat_axis=0, tiled=True
    )
    up = [(i, (i + 1) % planes) for i in range(planes)]
    down = [(i, (i - 1) % planes) for i in range(planes)]
    low = lax.ppermute(back[:half], "x", up)
    high = lax.ppermute(back[half:], "x", down)
    held = place_own(side_ref, back, blocks)
    return place_others(side_ref, held, low, high)


def solution(mesh):
    fine = Mesh(mesh.devices.reshape(64, 2, 4), ("yz", "c", "x"))
    rows = P(None, ("yz", "c"), None)
    return jax.shard_map(body, mesh=fine, in_specs=(rows, P(), P()), out_specs=rows, check_vma=False)
```

```python
import functools

import jax
import jax.numpy as jnp
from jax import lax
from jax.experimental import pallas as pl
from jax.experimental.pallas import tpu as pltpu
from jax.sharding import Mesh
from jax.sharding import PartitionSpec as P

EPS = 1e-06
TILE = 256
HANDED = (0, 4, 8, 12, 16, 24, 32)
BLOCK, RANK, TIER, PAIR, COUNT = range(5)


def down_columns(row):
    n = row.shape[1]
    return jnp.broadcast_to(row, (n, n)).T


def plan_kernel(side_ref, owners_ref, counts_ref, grads_ref, out_ref, plan_ref, rows_ref, plan_sem, sem):
    places, blocks = out_ref.shape[0], owners_ref.shape[1]
    square = (blocks, blocks)
    i = lax.broadcasted_iota(jnp.int32, square, 0)
    j = lax.broadcasted_iota(jnp.int32, square, 1)
    owners = jnp.broadcast_to(owners_ref[...], square)
    same = (down_columns(owners_ref[...]) == owners) & (i < j)
    slot = jnp.sum(jnp.where(same, 1, 0), axis=0, keepdims=True)
    have = jnp.sum(jnp.where(owners == i, down_columns(counts_ref[...]), 0), axis=0, keepdims=True)
    valid = jnp.where(slot < have, 1, 0)
    before = jnp.sum(jnp.where(i < j, down_columns(valid), 0), axis=0, keepdims=True)
    rank = jnp.where(slot < have, before, -1)
    block = jnp.sum(jnp.where(down_columns(rank) == j, i, 0), axis=0, keepdims=True)
    count = jnp.broadcast_to(jnp.sum(valid, axis=1, keepdims=True), (1, blocks))
    tier, pair = jnp.zeros_like(count), jnp.zeros_like(count)
    for smaller, k in zip(HANDED, HANDED[1:]):
        more = count > places + 2 * smaller
        tier = jnp.where(more, tier + 1, tier)
        pair = jnp.where(more, 2 * k, pair)
    for index, row in ((BLOCK, block), (RANK, rank), (TIER, tier), (PAIR, pair), (COUNT, count)):
        rows_ref[index : index + 1, :] = row
    to_scalars = pltpu.make_async_copy(rows_ref, plan_ref, plan_sem)
    to_scalars.start()
    to_scalars.wait()

    pair = plan_ref[PAIR, 0]
    first = side_ref[0] * pair

    def pick(place, carry):
        position = jnp.where(place < first, place, place + pair)
        pltpu.make_async_copy(grads_ref.at[plan_ref[BLOCK, position]], out_ref.at[place], sem).start()
        return carry

    lax.fori_loop(0, places, pick, 0, unroll=8)
    pltpu.make_async_copy(out_ref, out_ref, sem).wait()


def make_plan(side, owners, counts, grads, places):
    blocks = grads.shape[0]
    vmem = pl.BlockSpec(memory_space=pltpu.VMEM)
    smem = pl.BlockSpec(memory_space=pltpu.SMEM)
    return pl.pallas_call(
        plan_kernel,
        out_shape=(
            jax.ShapeDtypeStruct((places,) + grads.shape[1:], grads.dtype),
            jax.ShapeDtypeStruct((8, blocks), jnp.int32),
        ),
        in_specs=[smem, vmem, vmem, pl.BlockSpec(memory_space=pltpu.HBM)],
        out_specs=(vmem, smem),
        scratch_shapes=[
            pltpu.VMEM((8, blocks), jnp.int32),
            pltpu.SemaphoreType.DMA,
            pltpu.SemaphoreType.DMA,
        ],
    )(side, owners.reshape(1, -1), counts.reshape(1, -1), grads)


def first_dims(a, b):
    return lax.dot_general(a, b, (((0,), (0,)), ((), ())), preferred_element_type=jnp.float32)


def gram_kernel(rows_ref, out_ref):
    width = rows_ref.shape[1]
    for j in range(0, width, TILE):
        out_ref[j:, j : j + TILE] = first_dims(rows_ref[:, j:], rows_ref[:, j : j + TILE])


def gram(rows):
    count, width = rows.shape
    vmem = pl.BlockSpec(memory_space=pltpu.VMEM)
    return pl.pallas_call(
        gram_kernel,
        out_shape=jax.ShapeDtypeStruct((width, width), jnp.float32),
        in_specs=[vmem],
        out_specs=vmem,
        compiler_params=pltpu.CompilerParams(vmem_limit_bytes=24 * 2**20),
        cost_estimate=pl.CostEstimate(
            flops=2 * count * width**2, bytes_accessed=2 * count * width + 4 * width**2, transcendentals=0
        ),
    )(rows)


def on_diagonal(tile):
    r = lax.broadcasted_iota(jnp.int32, tile.shape, 0)
    c = lax.broadcasted_iota(jnp.int32, tile.shape, 1)
    return r == c


def refresh_kernel(mine_ref, theirs_ref, gram_ref, out_ref, right, root_r, rest, product):
    rows, width = mine_ref.shape
    total_sq = jnp.zeros((1, 1), jnp.float32)
    for j in range(0, width, TILE):
        tile = gram_ref[j:, j : j + TILE] + first_dims(theirs_ref[:, j:], theirs_ref[:, j : j + TILE])
        right[j:, j : j + TILE] = tile
        top = tile[:TILE, :]
        total_sq += jnp.sum(jnp.where(on_diagonal(top), top, 0.0), keepdims=True)

    scale_c = total_sq / width + EPS
    quarter = lax.rsqrt(jnp.sqrt(scale_c)) * 0.25
    slope = quarter / scale_c
    diag = 5.0 * quarter - EPS * slope
    for j in range(0, width, TILE):
        cols = slice(j, j + TILE)
        tile = -slope * right[cols, cols]
        tile = jnp.where(on_diagonal(tile), diag + tile, tile)
        kept = tile.astype(jnp.bfloat16)
        root_r[cols, cols] = kept
        off = jnp.where(on_diagonal(tile), tile - kept.astype(jnp.float32), 0.0)
        rest[:, cols] = 2.0 * jnp.sum(off, axis=0, keepdims=True)
        if j + TILE < width:
            below = (-slope * right[j + TILE :, cols]).astype(jnp.bfloat16)
            root_r[j + TILE :, cols] = below
            root_r[cols, j + TILE :] = below.T

    product_sq = jnp.zeros((1, 1), jnp.float32)
    for ref, keep in ((mine_ref, True), (theirs_ref, False)):
        for i in range(0, rows, TILE):
            hidden = jnp.dot(ref[i : i + TILE, :], root_r[...], preferred_element_type=jnp.float32)
            done = jnp.dot(hidden.astype(jnp.bfloat16), root_r[...], preferred_element_type=jnp.float32)
            done = done + hidden * rest[...]
            product_sq += jnp.sum(done * done, keepdims=True)
            if keep:
                product[i : i + TILE, :] = done
    graft = jnp.sqrt((total_sq + EPS) / (product_sq + EPS))
    out_ref[...] = (product[...] * graft).astype(jnp.bfloat16)


def refresh(mine, theirs, mine_gram):
    rows, width = mine.shape
    vmem = pl.BlockSpec(memory_space=pltpu.VMEM)
    return pl.pallas_call(
        refresh_kernel,
        out_shape=jax.ShapeDtypeStruct((rows, width), jnp.bfloat16),
        in_specs=[vmem, vmem, vmem],
        out_specs=vmem,
        scratch_shapes=[
            pltpu.VMEM((width, width), jnp.float32),
            pltpu.VMEM((width, width), jnp.bfloat16),
            pltpu.VMEM((1, width), jnp.float32),
            pltpu.VMEM((rows, width), jnp.float32),
        ],
        compiler_params=pltpu.CompilerParams(vmem_limit_bytes=40 * 2**20),
        cost_estimate=pl.CostEstimate(flops=5 * width**3, bytes_accessed=6 * rows * width, transcendentals=0),
    )(mine, theirs, mine_gram)


def place_own_kernel(side_ref, plan_ref, own_ref, out_ref, whole, sems):
    blocks = out_ref.shape[0]
    pieces = sems.shape[0]
    piece = blocks // pieces
    pair = plan_ref[PAIR, 0]
    first = side_ref[0] * pair
    copies = []
    for p in range(pieces):
        for block in range(p * piece, (p + 1) * piece):
            rank = plan_ref[RANK, block]
            place = jnp.where(rank < first, rank, rank - pair)
            held = (rank >= 0) & ((rank < first) | (rank >= first + pair))
            rows = own_ref[jnp.where(held, place, 0)]
            whole[block] = jnp.where(held, rows, jnp.zeros_like(rows))
        part = pl.ds(p * piece, piece)
        copies.append(pltpu.make_async_copy(whole.at[part], out_ref.at[part], sems.at[p]))
        copies[-1].start()
    for copy in copies:
        copy.wait()


def place_own(side, plan, own):
    blocks = plan.shape[1]
    shape = (blocks,) + own.shape[1:]
    smem = pl.BlockSpec(memory_space=pltpu.SMEM)
    return pl.pallas_call(
        place_own_kernel,
        out_shape=jax.ShapeDtypeStruct(shape, own.dtype),
        in_specs=[smem, smem, pl.BlockSpec(memory_space=pltpu.VMEM)],
        out_specs=pl.BlockSpec(memory_space=pltpu.HBM),
        scratch_shapes=[pltpu.VMEM(shape, own.dtype), pltpu.SemaphoreType.DMA((8,))],
        cost_estimate=pl.CostEstimate(flops=0, bytes_accessed=4 * own.size, transcendentals=0),
    )(side, plan, own)


def place_others_kernel(side_ref, plan_ref, held_ref, low_ref, high_ref, out_ref, sems):
    k = low_ref.shape[0]
    first = side_ref[0] * (2 * k)
    count = plan_ref[COUNT, 0]
    copies = []
    for q in range(2 * k):
        source = low_ref.at[q] if q < k else high_ref.at[q - k]
        copies.append(pltpu.make_async_copy(source, out_ref.at[plan_ref[BLOCK, first + q]], sems.at[q]))
    for act in ("start", "wait"):
        for q, copy in enumerate(copies):
            pl.when(first + q < count)(getattr(copy, act))


def place_others(side, plan, held, low, high):
    smem = pl.BlockSpec(memory_space=pltpu.SMEM)
    vmem = pl.BlockSpec(memory_space=pltpu.VMEM)
    hbm = pl.BlockSpec(memory_space=pltpu.HBM)
    return pl.pallas_call(
        place_others_kernel,
        out_shape=jax.ShapeDtypeStruct(held.shape, held.dtype),
        in_specs=[smem, smem, hbm, vmem, vmem],
        out_specs=hbm,
        scratch_shapes=[pltpu.SemaphoreType.DMA((2 * low.shape[0],))],
        input_output_aliases={2: 0},
        cost_estimate=pl.CostEstimate(flops=0, bytes_accessed=8 * low.size, transcendentals=0),
    )(side, plan, held, low, high)


def exchange(k, side, plan, own):
    planes = lax.axis_size("x")
    if k == 0:
        return place_own(side, plan, own)
    up = [(i, (i + 1) % planes) for i in range(planes)]
    down = [(i, (i - 1) % planes) for i in range(planes)]
    low = lax.ppermute(own[:k], "x", up)
    high = lax.ppermute(own[k : 2 * k], "x", down)
    held = place_own(side, plan, own)
    return place_others(side, plan, held, low, high)


def body(grads, owners, counts):
    blocks, rows_dev, width = grads.shape
    chips = lax.axis_size("yz")
    side = (lax.axis_index("x") % 2).astype(jnp.int32).reshape(1)

    outgoing, plan = make_plan(side, owners, counts, grads, chips)
    mine = lax.all_to_all(outgoing, "yz", split_axis=0, concat_axis=0, tiled=True)
    mine = mine.reshape(chips * rows_dev, width)
    theirs = lax.ppermute(mine, "c", [(0, 1), (1, 0)])
    done = refresh(mine, theirs, gram(mine))
    own = lax.all_to_all(
        done.reshape(chips, rows_dev, width), "yz", split_axis=0, concat_axis=0, tiled=True
    )
    branches = [functools.partial(exchange, k) for k in HANDED]
    return lax.switch(plan[TIER, 0], branches, side, plan, own)


def solution(mesh):
    fine = Mesh(mesh.devices.reshape(64, 2, 4), ("yz", "c", "x"))
    rows = P(None, ("yz", "c"), None)
    return jax.shard_map(body, mesh=fine, in_specs=(rows, P(), P()), out_specs=rows, check_vma=False)
```

```python
import functools

import jax
import jax.numpy as jnp
from jax import lax
from jax.experimental import pallas as pl
from jax.experimental.pallas import tpu as pltpu
from jax.sharding import Mesh
from jax.sharding import PartitionSpec as P

EPS = 1e-06
TILE = 256
HANDED = ((0, 0), (8, 0), (13, 3), (17, 7), (21, 11), (29, 19), (37, 27))
BLOCK, RANK, TIER, MORE, COUNT = range(5)


def down_columns(row):
    n = row.shape[1]
    return jnp.broadcast_to(row, (n, n)).T


def plan_kernel(
    side_ref, owners_ref, counts_ref, grads_ref, out_ref, plan_ref, whole, rows_ref, plan_sem, whole_sem
):
    load = pltpu.make_async_copy(grads_ref, whole, whole_sem)
    load.start()
    places, blocks = out_ref.shape[0], owners_ref.shape[1]
    square = (blocks, blocks)
    i = lax.broadcasted_iota(jnp.int32, square, 0)
    j = lax.broadcasted_iota(jnp.int32, square, 1)
    owners = jnp.broadcast_to(owners_ref[...], square)
    same = (down_columns(owners_ref[...]) == owners) & (i < j)
    slot = jnp.sum(jnp.where(same, 1, 0), axis=0, keepdims=True)
    have = jnp.sum(jnp.where(owners == i, down_columns(counts_ref[...]), 0), axis=0, keepdims=True)
    valid = jnp.where(slot < have, 1, 0)
    before = jnp.sum(jnp.where(i < j, down_columns(valid), 0), axis=0, keepdims=True)
    count = jnp.broadcast_to(jnp.sum(valid, axis=1, keepdims=True), (1, blocks))
    rank = jnp.where(slot < have, before, count + j[:1, :] - before)
    block = jnp.sum(jnp.where(down_columns(rank) == j, i, 0), axis=0, keepdims=True)
    tier, more = jnp.zeros_like(count), jnp.zeros_like(count)
    for smaller, larger in zip(HANDED, HANDED[1:]):
        above = count > places + sum(smaller)
        tier = jnp.where(above, tier + 1, tier)
        more = jnp.where(above, sum(larger), more)
    for index, row in ((BLOCK, block), (RANK, rank), (TIER, tier), (MORE, more), (COUNT, count)):
        rows_ref[index : index + 1, :] = row
    to_scalars = pltpu.make_async_copy(rows_ref, plan_ref, plan_sem)
    to_scalars.start()
    to_scalars.wait()
    load.wait()
    more = plan_ref[MORE, 0]
    first = side_ref[0] * more
    for place in range(places):
        position = jnp.where(place < first, place, place + more)
        out_ref[place] = whole[plan_ref[BLOCK, position]]


def make_plan(side, owners, counts, grads, places):
    blocks = grads.shape[0]
    vmem = pl.BlockSpec(memory_space=pltpu.VMEM)
    smem = pl.BlockSpec(memory_space=pltpu.SMEM)
    return pl.pallas_call(
        plan_kernel,
        out_shape=(
            jax.ShapeDtypeStruct((places,) + grads.shape[1:], grads.dtype),
            jax.ShapeDtypeStruct((8, blocks), jnp.int32),
        ),
        in_specs=[smem, vmem, vmem, pl.BlockSpec(memory_space=pltpu.HBM)],
        out_specs=(vmem, smem),
        scratch_shapes=[
            pltpu.VMEM(grads.shape, grads.dtype),
            pltpu.VMEM((8, blocks), jnp.int32),
            pltpu.SemaphoreType.DMA,
            pltpu.SemaphoreType.DMA,
        ],
    )(side, owners.reshape(1, -1), counts.reshape(1, -1), grads)


def first_dims(a, b):
    return lax.dot_general(a, b, (((0,), (0,)), ((), ())), preferred_element_type=jnp.float32)


def gram_kernel(rows_ref, out_ref):
    width = rows_ref.shape[1]
    for j in range(0, width, TILE):
        out_ref[j:, j : j + TILE] = first_dims(rows_ref[:, j:], rows_ref[:, j : j + TILE])


def gram(rows):
    count, width = rows.shape
    vmem = pl.BlockSpec(memory_space=pltpu.VMEM)
    return pl.pallas_call(
        gram_kernel,
        out_shape=jax.ShapeDtypeStruct((width, width), jnp.float32),
        in_specs=[vmem],
        out_specs=vmem,
        compiler_params=pltpu.CompilerParams(vmem_limit_bytes=24 * 2**20),
        cost_estimate=pl.CostEstimate(
            flops=2 * count * width**2, bytes_accessed=2 * count * width + 4 * width**2, transcendentals=0
        ),
    )(rows)


def on_diagonal(tile):
    r = lax.broadcasted_iota(jnp.int32, tile.shape, 0)
    c = lax.broadcasted_iota(jnp.int32, tile.shape, 1)
    return r == c


def folded_squares(tile):
    squares = tile * tile
    folded = jnp.sum(squares.reshape(tile.shape[0] // 8, 8, tile.shape[1]), axis=0)
    return sum(folded[:, c : c + 128] for c in range(0, tile.shape[1], 128))


def refresh_kernel(
    side_ref, plan_ref, mine_ref, theirs_ref, gram_ref, out_ref, right, root, square, rest, product
):
    rows, width = mine_ref.shape
    place, more = side_ref[1], plan_ref[MORE, 0]
    position = jnp.where(place < side_ref[0] * more, place, place + more)
    valid = jnp.where(position < plan_ref[COUNT, 0], 1.0, 0.0)

    total_sq = jnp.zeros((1, 1), jnp.float32)
    for j in range(0, width, TILE):
        tile = gram_ref[j:, j : j + TILE] + first_dims(theirs_ref[:, j:], theirs_ref[:, j : j + TILE])
        right[j:, j : j + TILE] = tile
        top = tile[:TILE, :]
        total_sq += jnp.sum(jnp.where(on_diagonal(top), top, 0.0), keepdims=True)

    scale_c = total_sq / width + EPS
    quarter = lax.rsqrt(jnp.sqrt(scale_c)) * 0.25
    slope = quarter / scale_c
    diag = 5.0 * quarter - EPS * slope
    for j in range(0, width, TILE):
        cols = slice(j, j + TILE)
        tile = -slope * right[cols, cols]
        tile = jnp.where(on_diagonal(tile), diag + tile, tile)
        kept = tile.astype(jnp.bfloat16)
        root[cols, cols] = kept
        kept = kept.astype(jnp.float32)
        off = jnp.where(on_diagonal(tile), 2.0 * (tile - kept) * kept, 0.0)
        rest[:, cols] = jnp.sum(off, axis=0, keepdims=True)
        if j + TILE < width:
            below = (-slope * right[j + TILE :, cols]).astype(jnp.bfloat16)
            root[j + TILE :, cols] = below
            root[cols, j + TILE :] = below.T

    for j in range(0, width, TILE):
        cols = slice(j, j + TILE)
        tile = jnp.dot(root[j:, :], root[:, cols], preferred_element_type=jnp.float32)
        top = tile[:TILE]
        kept = top.astype(jnp.bfloat16)
        square[cols, cols] = kept
        off = jnp.where(on_diagonal(top), top - kept.astype(jnp.float32), 0.0)
        rest[:, cols] += jnp.sum(off, axis=0, keepdims=True)
        if j + TILE < width:
            below = tile[TILE:].astype(jnp.bfloat16)
            square[j + TILE :, cols] = below
            square[cols, j + TILE :] = below.T

    squares = jnp.zeros((8, 128), jnp.float32)
    for ref, keep in ((mine_ref, True), (theirs_ref, False)):
        for j in range(0, width, TILE):
            cols = slice(j, j + TILE)
            done = jnp.dot(ref[...], square[:, cols], preferred_element_type=jnp.float32)
            done = done + ref[:, cols].astype(jnp.float32) * rest[:, cols]
            squares += folded_squares(done)
            if keep:
                product[:, cols] = done
    product_sq = jnp.sum(squares, keepdims=True)
    graft = jnp.sqrt((total_sq + EPS) / (product_sq + EPS)) * valid
    out_ref[...] = (product[...] * graft).astype(jnp.bfloat16)


def refresh(side, plan, mine, theirs, mine_gram):
    rows, width = mine.shape
    vmem = pl.BlockSpec(memory_space=pltpu.VMEM)
    smem = pl.BlockSpec(memory_space=pltpu.SMEM)
    return pl.pallas_call(
        refresh_kernel,
        out_shape=jax.ShapeDtypeStruct((rows, width), jnp.bfloat16),
        in_specs=[smem, smem, vmem, vmem, vmem],
        out_specs=vmem,
        scratch_shapes=[
            pltpu.VMEM((width, width), jnp.float32),
            pltpu.VMEM((width, width), jnp.bfloat16),
            pltpu.VMEM((width, width), jnp.bfloat16),
            pltpu.VMEM((1, width), jnp.float32),
            pltpu.VMEM((rows, width), jnp.float32),
        ],
        compiler_params=pltpu.CompilerParams(vmem_limit_bytes=44 * 2**20),
        cost_estimate=pl.CostEstimate(flops=4 * width**3, bytes_accessed=6 * rows * width, transcendentals=0),
    )(side, plan, mine, theirs, mine_gram)


def place_own_kernel(side_ref, plan_ref, own_ref, out_ref, whole, sems):
    blocks = out_ref.shape[0]
    pieces = sems.shape[0]
    piece = blocks // pieces
    more, count = plan_ref[MORE, 0], plan_ref[COUNT, 0]
    first = side_ref[0] * more
    copies = []
    for p in range(pieces):
        for block in range(p * piece, (p + 1) * piece):
            rank = plan_ref[RANK, block]
            place = jnp.where(rank < first, rank, rank - more)
            held = (rank < count) & ((rank < first) | (rank >= first + more))
            rows = own_ref[jnp.where(held, place, 0)]
            whole[block] = jnp.where(held, rows, jnp.zeros_like(rows))
        part = pl.ds(p * piece, piece)
        copies.append(pltpu.make_async_copy(whole.at[part], out_ref.at[part], sems.at[p]))
        copies[-1].start()
    for copy in copies:
        copy.wait()


def place_own(side, plan, own):
    blocks = plan.shape[1]
    shape = (blocks,) + own.shape[1:]
    smem = pl.BlockSpec(memory_space=pltpu.SMEM)
    return pl.pallas_call(
        place_own_kernel,
        out_shape=jax.ShapeDtypeStruct(shape, own.dtype),
        in_specs=[smem, smem, pl.BlockSpec(memory_space=pltpu.VMEM)],
        out_specs=pl.BlockSpec(memory_space=pltpu.HBM),
        scratch_shapes=[pltpu.VMEM(shape, own.dtype), pltpu.SemaphoreType.DMA((8,))],
        cost_estimate=pl.CostEstimate(flops=0, bytes_accessed=4 * own.size, transcendentals=0),
    )(side, plan, own)


def place_others_kernel(side_ref, plan_ref, held_ref, *refs):
    parts, out_ref, sems = refs[:-2], refs[-2], refs[-1]
    position = side_ref[0] * sum(part.shape[0] for part in parts)
    for index, part in enumerate(parts):
        for q in range(part.shape[0]):
            target = out_ref.at[plan_ref[BLOCK, position + q]]
            pltpu.make_async_copy(part.at[q], target, sems.at[index]).start()
        position += part.shape[0]
    for index, part in enumerate(parts):
        pltpu.make_async_copy(part, part, sems.at[index]).wait()


def place_others(side, plan, held, parts):
    smem = pl.BlockSpec(memory_space=pltpu.SMEM)
    vmem = pl.BlockSpec(memory_space=pltpu.VMEM)
    hbm = pl.BlockSpec(memory_space=pltpu.HBM)
    size = sum(part.size for part in parts)
    return pl.pallas_call(
        place_others_kernel,
        out_shape=jax.ShapeDtypeStruct(held.shape, held.dtype),
        in_specs=[smem, smem, hbm] + [vmem] * len(parts),
        out_specs=hbm,
        scratch_shapes=[pltpu.SemaphoreType.DMA((len(parts),))],
        input_output_aliases={2: 0},
        cost_estimate=pl.CostEstimate(flops=0, bytes_accessed=4 * size, transcendentals=0),
    )(side, plan, held, *parts)


def exchange(handed, side, plan, own):
    planes = lax.axis_size("x")
    start, parts = 0, []
    for size, step in zip(handed, (1, -1)):
        if size:
            pairs = [(i, (i + step) % planes) for i in range(planes)]
            parts.append(lax.ppermute(own[start : start + size], "x", pairs))
            start += size
    held = place_own(side, plan, own)
    return place_others(side, plan, held, parts) if parts else held


def body(grads, owners, counts):
    blocks, rows_dev, width = grads.shape
    chips = lax.axis_size("yz")
    side = jnp.stack([lax.axis_index("x") % 2, lax.axis_index("yz")]).astype(jnp.int32)

    outgoing, plan = make_plan(side, owners, counts, grads, chips)
    mine = lax.all_to_all(outgoing, "yz", split_axis=0, concat_axis=0, tiled=True)
    mine = mine.reshape(chips * rows_dev, width)
    theirs = lax.ppermute(mine, "c", [(0, 1), (1, 0)])
    done = refresh(side, plan, mine, theirs, gram(mine))
    own = lax.all_to_all(
        done.reshape(chips, rows_dev, width), "yz", split_axis=0, concat_axis=0, tiled=True
    )
    branches = [functools.partial(exchange, handed) for handed in HANDED]
    return lax.switch(plan[TIER, 0], branches, side, plan, own)


def solution(mesh):
    fine = Mesh(mesh.devices.reshape(64, 2, 4), ("yz", "c", "x"))
    rows = P(None, ("yz", "c"), None)
    return jax.shard_map(body, mesh=fine, in_specs=(rows, P(), P()), out_specs=rows, check_vma=False)
```

```python
import functools

import jax
import jax.numpy as jnp
from jax import lax
from jax.experimental import pallas as pl
from jax.experimental.pallas import tpu as pltpu
from jax.sharding import Mesh
from jax.sharding import PartitionSpec as P

EPS = 1e-06
TILE = 256
HANDED = ((0, 0), (8, 0), (13, 3), (17, 7), (21, 11), (29, 19), (37, 27))
BLOCK, RANK, TIER, MORE, COUNT = range(5)


def down_columns(row):
    n = row.shape[1]
    return jnp.broadcast_to(row, (n, n)).T


def plan_kernel(
    side_ref, owners_ref, counts_ref, grads_ref, out_ref, plan_ref, whole, rows_ref, plan_sem, whole_sems
):
    piece = whole.shape[0] // whole_sems.shape[0]
    loads = []
    for p in range(whole_sems.shape[0]):
        part = pl.ds(p * piece, piece)
        loads.append(pltpu.make_async_copy(grads_ref.at[part], whole.at[part], whole_sems.at[p]))
        loads[-1].start()
    places, blocks = out_ref.shape[0], owners_ref.shape[1]
    square = (blocks, blocks)
    i = lax.broadcasted_iota(jnp.int32, square, 0)
    j = lax.broadcasted_iota(jnp.int32, square, 1)
    owners = jnp.broadcast_to(owners_ref[...], square)
    same = (down_columns(owners_ref[...]) == owners) & (i < j)
    slot = jnp.sum(jnp.where(same, 1, 0), axis=0, keepdims=True)
    have = jnp.sum(jnp.where(owners == i, down_columns(counts_ref[...]), 0), axis=0, keepdims=True)
    valid = jnp.where(slot < have, 1, 0)
    before = jnp.sum(jnp.where(i < j, down_columns(valid), 0), axis=0, keepdims=True)
    count = jnp.broadcast_to(jnp.sum(valid, axis=1, keepdims=True), (1, blocks))
    rank = jnp.where(slot < have, before, count + j[:1, :] - before)
    block = jnp.sum(jnp.where(down_columns(rank) == j, i, 0), axis=0, keepdims=True)
    tier, more = jnp.zeros_like(count), jnp.zeros_like(count)
    for smaller, larger in zip(HANDED, HANDED[1:]):
        above = count > places + sum(smaller)
        tier = jnp.where(above, tier + 1, tier)
        more = jnp.where(above, sum(larger), more)
    for index, row in ((BLOCK, block), (RANK, rank), (TIER, tier), (MORE, more), (COUNT, count)):
        rows_ref[index : index + 1, :] = row
    to_scalars = pltpu.make_async_copy(rows_ref, plan_ref, plan_sem)
    to_scalars.start()
    to_scalars.wait()
    for load in loads:
        load.wait()
    more = plan_ref[MORE, 0]
    first = side_ref[0] * more
    for place in range(places):
        position = jnp.where(place < first, place, place + more)
        out_ref[place] = whole[plan_ref[BLOCK, position]]


def make_plan(side, owners, counts, grads, places):
    blocks = grads.shape[0]
    vmem = pl.BlockSpec(memory_space=pltpu.VMEM)
    smem = pl.BlockSpec(memory_space=pltpu.SMEM)
    return pl.pallas_call(
        plan_kernel,
        out_shape=(
            jax.ShapeDtypeStruct((places,) + grads.shape[1:], grads.dtype),
            jax.ShapeDtypeStruct((8, blocks), jnp.int32),
        ),
        in_specs=[smem, vmem, vmem, pl.BlockSpec(memory_space=pltpu.HBM)],
        out_specs=(vmem, smem),
        scratch_shapes=[
            pltpu.VMEM(grads.shape, grads.dtype),
            pltpu.VMEM((8, blocks), jnp.int32),
            pltpu.SemaphoreType.DMA,
            pltpu.SemaphoreType.DMA((8,)),
        ],
        compiler_params=pltpu.CompilerParams(vmem_limit_bytes=8 * 2**20),
    )(side, owners.reshape(1, -1), counts.reshape(1, -1), grads)


def first_dims(a, b):
    return lax.dot_general(a, b, (((0,), (0,)), ((), ())), preferred_element_type=jnp.float32)


def gram_kernel(rows_ref, out_ref):
    width = rows_ref.shape[1]
    for j in range(0, width, TILE):
        out_ref[j:, j : j + TILE] = first_dims(rows_ref[:, j:], rows_ref[:, j : j + TILE])


def gram(rows):
    count, width = rows.shape
    vmem = pl.BlockSpec(memory_space=pltpu.VMEM)
    return pl.pallas_call(
        gram_kernel,
        out_shape=jax.ShapeDtypeStruct((width, width), jnp.float32),
        in_specs=[vmem],
        out_specs=vmem,
        compiler_params=pltpu.CompilerParams(vmem_limit_bytes=12 * 2**20),
        cost_estimate=pl.CostEstimate(
            flops=2 * count * width**2, bytes_accessed=2 * count * width + 4 * width**2, transcendentals=0
        ),
    )(rows)


def on_diagonal(tile):
    r = lax.broadcasted_iota(jnp.int32, tile.shape, 0)
    c = lax.broadcasted_iota(jnp.int32, tile.shape, 1)
    return r == c


def folded_squares(tile):
    squares = tile * tile
    folded = jnp.sum(squares.reshape(tile.shape[0] // 8, 8, tile.shape[1]), axis=0)
    return sum(folded[:, c : c + 128] for c in range(0, tile.shape[1], 128))


def refresh_kernel(
    side_ref, plan_ref, mine_ref, theirs_ref, gram_ref, out_ref, right, root, square, rest, product
):
    rows, width = mine_ref.shape
    place, more = side_ref[1], plan_ref[MORE, 0]
    position = jnp.where(place < side_ref[0] * more, place, place + more)
    valid = jnp.where(position < plan_ref[COUNT, 0], 1.0, 0.0)

    total_sq = jnp.zeros((1, 1), jnp.float32)
    for j in range(0, width, TILE):
        tile = gram_ref[j:, j : j + TILE] + first_dims(theirs_ref[:, j:], theirs_ref[:, j : j + TILE])
        right[j:, j : j + TILE] = tile
        top = tile[:TILE, :]
        total_sq += jnp.sum(jnp.where(on_diagonal(top), top, 0.0), keepdims=True)

    scale_c = total_sq / width + EPS
    quarter = lax.rsqrt(jnp.sqrt(scale_c)) * 0.25
    slope = quarter / scale_c
    diag = 5.0 * quarter - EPS * slope
    for j in range(0, width, TILE):
        cols = slice(j, j + TILE)
        tile = -slope * right[cols, cols]
        tile = jnp.where(on_diagonal(tile), diag + tile, tile)
        kept = tile.astype(jnp.bfloat16)
        root[cols, cols] = kept
        kept = kept.astype(jnp.float32)
        off = jnp.where(on_diagonal(tile), 2.0 * (tile - kept) * kept, 0.0)
        rest[:, cols] = jnp.sum(off, axis=0, keepdims=True)
        if j + TILE < width:
            below = (-slope * right[j + TILE :, cols]).astype(jnp.bfloat16)
            root[j + TILE :, cols] = below
            root[cols, j + TILE :] = below.T

    for j in range(0, width, TILE):
        cols = slice(j, j + TILE)
        tile = jnp.dot(root[j:, :], root[:, cols], preferred_element_type=jnp.float32)
        top = tile[:TILE]
        kept = top.astype(jnp.bfloat16)
        square[cols, cols] = kept
        off = jnp.where(on_diagonal(top), top - kept.astype(jnp.float32), 0.0)
        rest[:, cols] += jnp.sum(off, axis=0, keepdims=True)
        if j + TILE < width:
            below = tile[TILE:].astype(jnp.bfloat16)
            square[j + TILE :, cols] = below
            square[cols, j + TILE :] = below.T

    squares = jnp.zeros((8, 128), jnp.float32)
    for ref, keep in ((mine_ref, True), (theirs_ref, False)):
        for j in range(0, width, TILE):
            cols = slice(j, j + TILE)
            done = jnp.dot(ref[...], square[:, cols], preferred_element_type=jnp.float32)
            done = done + ref[:, cols].astype(jnp.float32) * rest[:, cols]
            squares += folded_squares(done)
            if keep:
                product[:, cols] = done
    product_sq = jnp.sum(squares, keepdims=True)
    graft = jnp.sqrt((total_sq + EPS) / (product_sq + EPS)) * valid
    out_ref[...] = (product[...] * graft).astype(jnp.bfloat16)


def refresh(side, plan, mine, theirs, mine_gram):
    rows, width = mine.shape
    vmem = pl.BlockSpec(memory_space=pltpu.VMEM)
    smem = pl.BlockSpec(memory_space=pltpu.SMEM)
    return pl.pallas_call(
        refresh_kernel,
        out_shape=jax.ShapeDtypeStruct((rows, width), jnp.bfloat16),
        in_specs=[smem, smem, vmem, vmem, vmem],
        out_specs=vmem,
        scratch_shapes=[
            pltpu.VMEM((width, width), jnp.float32),
            pltpu.VMEM((width, width), jnp.bfloat16),
            pltpu.VMEM((width, width), jnp.bfloat16),
            pltpu.VMEM((1, width), jnp.float32),
            pltpu.VMEM((rows, width), jnp.float32),
        ],
        compiler_params=pltpu.CompilerParams(vmem_limit_bytes=24 * 2**20),
        cost_estimate=pl.CostEstimate(flops=4 * width**3, bytes_accessed=6 * rows * width, transcendentals=0),
    )(side, plan, mine, theirs, mine_gram)


def place_own_kernel(side_ref, plan_ref, own_ref, out_ref, whole, sems):
    blocks = out_ref.shape[0]
    pieces = sems.shape[0]
    piece = blocks // pieces
    more, count = plan_ref[MORE, 0], plan_ref[COUNT, 0]
    first = side_ref[0] * more
    copies = []
    for p in range(pieces):
        for block in range(p * piece, (p + 1) * piece):
            rank = plan_ref[RANK, block]
            place = jnp.where(rank < first, rank, rank - more)
            held = (rank < count) & ((rank < first) | (rank >= first + more))
            rows = own_ref[jnp.where(held, place, 0)]
            whole[block] = jnp.where(held, rows, jnp.zeros_like(rows))
        part = pl.ds(p * piece, piece)
        copies.append(pltpu.make_async_copy(whole.at[part], out_ref.at[part], sems.at[p]))
        copies[-1].start()
    for copy in copies:
        copy.wait()


def place_own(side, plan, own):
    blocks = plan.shape[1]
    shape = (blocks,) + own.shape[1:]
    smem = pl.BlockSpec(memory_space=pltpu.SMEM)
    return pl.pallas_call(
        place_own_kernel,
        out_shape=jax.ShapeDtypeStruct(shape, own.dtype),
        in_specs=[smem, smem, pl.BlockSpec(memory_space=pltpu.VMEM)],
        out_specs=pl.BlockSpec(memory_space=pltpu.HBM),
        scratch_shapes=[pltpu.VMEM(shape, own.dtype), pltpu.SemaphoreType.DMA((8,))],
        compiler_params=pltpu.CompilerParams(vmem_limit_bytes=8 * 2**20),
        cost_estimate=pl.CostEstimate(flops=0, bytes_accessed=4 * own.size, transcendentals=0),
    )(side, plan, own)


def place_others_kernel(side_ref, plan_ref, held_ref, *refs):
    parts, out_ref, sems = refs[:-2], refs[-2], refs[-1]
    position = side_ref[0] * sum(part.shape[0] for part in parts)
    for index, part in enumerate(parts):
        for q in range(part.shape[0]):
            target = out_ref.at[plan_ref[BLOCK, position + q]]
            pltpu.make_async_copy(part.at[q], target, sems.at[index]).start()
        position += part.shape[0]
    for index, part in enumerate(parts):
        pltpu.make_async_copy(part, part, sems.at[index]).wait()


def place_others(side, plan, held, parts):
    smem = pl.BlockSpec(memory_space=pltpu.SMEM)
    vmem = pl.BlockSpec(memory_space=pltpu.VMEM)
    hbm = pl.BlockSpec(memory_space=pltpu.HBM)
    size = sum(part.size for part in parts)
    return pl.pallas_call(
        place_others_kernel,
        out_shape=jax.ShapeDtypeStruct(held.shape, held.dtype),
        in_specs=[smem, smem, hbm] + [vmem] * len(parts),
        out_specs=hbm,
        scratch_shapes=[pltpu.SemaphoreType.DMA((len(parts),))],
        input_output_aliases={2: 0},
        compiler_params=pltpu.CompilerParams(vmem_limit_bytes=6 * 2**20),
        cost_estimate=pl.CostEstimate(flops=0, bytes_accessed=4 * size, transcendentals=0),
    )(side, plan, held, *parts)


def exchange(handed, side, plan, own):
    planes = lax.axis_size("x")
    start, parts = 0, []
    for size, step in zip(handed, (1, -1)):
        if size:
            pairs = [(i, (i + step) % planes) for i in range(planes)]
            parts.append(lax.ppermute(own[start : start + size], "x", pairs))
            start += size
    held = place_own(side, plan, own)
    return place_others(side, plan, held, parts) if parts else held


def body(grads, owners, counts):
    blocks, rows_dev, width = grads.shape
    chips = lax.axis_size("yz")
    side = jnp.stack([lax.axis_index("x") % 2, lax.axis_index("yz")]).astype(jnp.int32)

    outgoing, plan = make_plan(side, owners, counts, grads, chips)
    mine = lax.all_to_all(outgoing, "yz", split_axis=0, concat_axis=0, tiled=True)
    mine = mine.reshape(chips * rows_dev, width)
    theirs = lax.ppermute(mine, "c", [(0, 1), (1, 0)])
    done = refresh(side, plan, mine, theirs, gram(mine))
    own = lax.all_to_all(
        done.reshape(chips, rows_dev, width), "yz", split_axis=0, concat_axis=0, tiled=True
    )
    branches = [functools.partial(exchange, handed) for handed in HANDED]
    return lax.switch(plan[TIER, 0], branches, side, plan, own)


def solution(mesh):
    fine = Mesh(mesh.devices.reshape(64, 2, 4), ("yz", "c", "x"))
    rows = P(None, ("yz", "c"), None)
    return jax.shard_map(body, mesh=fine, in_specs=(rows, P(), P()), out_specs=rows, check_vma=False)
```

```python
import functools

import jax
import jax.numpy as jnp
from jax import lax
from jax.experimental import pallas as pl
from jax.experimental.pallas import tpu as pltpu
from jax.sharding import Mesh
from jax.sharding import PartitionSpec as P

EPS = 1e-06
TILE = 256
HANDED = (
    *((0, 0), (4, 0), (8, 0), (12, 0), (16, 0), (15, 5)),
    *((17, 7), (19, 9), (21, 11), (25, 15), (29, 19), (37, 27)),
)
BLOCK, RANK, TIER, MORE, COUNT = range(5)


def down_columns(row):
    n = row.shape[1]
    return jnp.broadcast_to(row, (n, n)).T


def plan_kernel(
    side_ref, owners_ref, counts_ref, grads_ref, out_ref, plan_ref, tier_ref, whole, rows_ref, plan_sem, whole_sems
):
    piece = whole.shape[0] // whole_sems.shape[0]
    loads = []
    for p in range(whole_sems.shape[0]):
        part = pl.ds(p * piece, piece)
        loads.append(pltpu.make_async_copy(grads_ref.at[part], whole.at[part], whole_sems.at[p]))
        loads[-1].start()
    places, blocks = out_ref.shape[0], owners_ref.shape[1]
    square = (blocks, blocks)
    i = lax.broadcasted_iota(jnp.int32, square, 0)
    j = lax.broadcasted_iota(jnp.int32, square, 1)
    owners = jnp.broadcast_to(owners_ref[...], square)
    same = (down_columns(owners_ref[...]) == owners) & (i < j)
    slot = jnp.sum(jnp.where(same, 1, 0), axis=0, keepdims=True)
    have = jnp.sum(jnp.where(owners == i, down_columns(counts_ref[...]), 0), axis=0, keepdims=True)
    valid = jnp.where(slot < have, 1, 0)
    before = jnp.sum(jnp.where(i < j, down_columns(valid), 0), axis=0, keepdims=True)
    count = jnp.broadcast_to(jnp.sum(valid, axis=1, keepdims=True), (1, blocks))
    rank = jnp.where(slot < have, before, count + j[:1, :] - before)
    block = jnp.sum(jnp.where(down_columns(rank) == j, i, 0), axis=0, keepdims=True)
    tier, more = jnp.zeros_like(count), jnp.zeros_like(count)
    for smaller, larger in zip(HANDED, HANDED[1:]):
        above = count > places + sum(smaller)
        tier = jnp.where(above, tier + 1, tier)
        more = jnp.where(above, sum(larger), more)
    for index, row in ((BLOCK, block), (RANK, rank), (TIER, tier), (MORE, more), (COUNT, count)):
        rows_ref[index : index + 1, :] = row
    to_scalars = pltpu.make_async_copy(rows_ref, plan_ref, plan_sem)
    to_scalars.start()
    to_scalars.wait()
    for load in loads:
        load.wait()
    tier_ref[0] = plan_ref[TIER, 0]
    more = plan_ref[MORE, 0]
    first = side_ref[0] * more
    for place in range(places):
        position = jnp.where(place < first, place, place + more)
        out_ref[place] = whole[plan_ref[BLOCK, position]]


def make_plan(side, owners, counts, grads, places):
    blocks = grads.shape[0]
    vmem = pl.BlockSpec(memory_space=pltpu.VMEM)
    smem = pl.BlockSpec(memory_space=pltpu.SMEM)
    return pl.pallas_call(
        plan_kernel,
        out_shape=(
            pltpu.VMEM((places,) + grads.shape[1:], grads.dtype),
            jax.ShapeDtypeStruct((8, blocks), jnp.int32),
            jax.ShapeDtypeStruct((1,), jnp.int32),
        ),
        in_specs=[smem, vmem, vmem, pl.BlockSpec(memory_space=pltpu.HBM)],
        out_specs=(vmem, smem, smem),
        scratch_shapes=[
            pltpu.VMEM(grads.shape, grads.dtype),
            pltpu.VMEM((8, blocks), jnp.int32),
            pltpu.SemaphoreType.DMA,
            pltpu.SemaphoreType.DMA((8,)),
        ],
        compiler_params=pltpu.CompilerParams(vmem_limit_bytes=8 * 2**20),
    )(
        side,
        *(
            pltpu.with_memory_space_constraint(array, pltpu.HBM)
            for array in (owners.reshape(1, -1), counts.reshape(1, -1), grads)
        ),
    )


def first_dims(a, b):
    return lax.dot_general(a, b, (((0,), (0,)), ((), ())), preferred_element_type=jnp.float32)


def gram_kernel(rows_ref, out_ref):
    width = rows_ref.shape[1]
    for j in range(0, width, TILE):
        out_ref[j:, j : j + TILE] = first_dims(rows_ref[:, j:], rows_ref[:, j : j + TILE])


def gram(rows):
    count, width = rows.shape
    vmem = pl.BlockSpec(memory_space=pltpu.VMEM)
    return pl.pallas_call(
        gram_kernel,
        out_shape=jax.ShapeDtypeStruct((width, width), jnp.float32),
        in_specs=[vmem],
        out_specs=vmem,
        compiler_params=pltpu.CompilerParams(vmem_limit_bytes=12 * 2**20),
        cost_estimate=pl.CostEstimate(
            flops=2 * count * width**2, bytes_accessed=2 * count * width + 4 * width**2, transcendentals=0
        ),
    )(rows)


def on_diagonal(tile):
    r = lax.broadcasted_iota(jnp.int32, tile.shape, 0)
    c = lax.broadcasted_iota(jnp.int32, tile.shape, 1)
    return r == c


def folded_squares(tile):
    squares = tile * tile
    folded = jnp.sum(squares.reshape(tile.shape[0] // 8, 8, tile.shape[1]), axis=0)
    return sum(folded[:, c : c + 128] for c in range(0, tile.shape[1], 128))


def refresh_kernel(
    side_ref, plan_ref, mine_ref, theirs_ref, gram_ref, out_ref, right, root, square, rest, product
):
    rows, width = mine_ref.shape
    place, more = side_ref[1], plan_ref[MORE, 0]
    position = jnp.where(place < side_ref[0] * more, place, place + more)
    valid = jnp.where(position < plan_ref[COUNT, 0], 1.0, 0.0)

    total_sq = jnp.zeros((1, 1), jnp.float32)
    for j in range(0, width, TILE):
        tile = gram_ref[j:, j : j + TILE] + first_dims(theirs_ref[:, j:], theirs_ref[:, j : j + TILE])
        right[j:, j : j + TILE] = tile
        top = tile[:TILE, :]
        total_sq += jnp.sum(jnp.where(on_diagonal(top), top, 0.0), keepdims=True)

    scale_c = total_sq / width + EPS
    quarter = lax.rsqrt(jnp.sqrt(scale_c)) * 0.25
    slope = quarter / scale_c
    diag = 5.0 * quarter - EPS * slope
    for j in range(0, width, TILE):
        cols = slice(j, j + TILE)
        tile = -slope * right[cols, cols]
        tile = jnp.where(on_diagonal(tile), diag + tile, tile)
        kept = tile.astype(jnp.bfloat16)
        root[cols, cols] = kept
        kept = kept.astype(jnp.float32)
        off = jnp.where(on_diagonal(tile), 2.0 * (tile - kept) * kept, 0.0)
        rest[:, cols] = jnp.sum(off, axis=0, keepdims=True)
        if j + TILE < width:
            below = (-slope * right[j + TILE :, cols]).astype(jnp.bfloat16)
            root[j + TILE :, cols] = below
            root[cols, j + TILE :] = below.T

    for j in range(0, width, TILE):
        cols = slice(j, j + TILE)
        tile = jnp.dot(root[j:, :], root[:, cols], preferred_element_type=jnp.float32)
        top = tile[:TILE]
        kept = top.astype(jnp.bfloat16)
        square[cols, cols] = kept
        off = jnp.where(on_diagonal(top), top - kept.astype(jnp.float32), 0.0)
        rest[:, cols] += jnp.sum(off, axis=0, keepdims=True)
        if j + TILE < width:
            below = tile[TILE:].astype(jnp.bfloat16)
            square[j + TILE :, cols] = below
            square[cols, j + TILE :] = below.T

    squares = jnp.zeros((8, 128), jnp.float32)
    for ref, keep in ((mine_ref, True), (theirs_ref, False)):
        for j in range(0, width, TILE):
            cols = slice(j, j + TILE)
            done = jnp.dot(ref[...], square[:, cols], preferred_element_type=jnp.float32)
            done = done + ref[:, cols].astype(jnp.float32) * rest[:, cols]
            squares += folded_squares(done)
            if keep:
                product[:, cols] = done
    product_sq = jnp.sum(squares, keepdims=True)
    graft = jnp.sqrt((total_sq + EPS) / (product_sq + EPS)) * valid
    out_ref[...] = (product[...] * graft).astype(jnp.bfloat16)


def refresh(side, plan, mine, theirs, mine_gram):
    rows, width = mine.shape
    vmem = pl.BlockSpec(memory_space=pltpu.VMEM)
    smem = pl.BlockSpec(memory_space=pltpu.SMEM)
    return pl.pallas_call(
        refresh_kernel,
        out_shape=jax.ShapeDtypeStruct((rows, width), jnp.bfloat16),
        in_specs=[smem, smem, vmem, vmem, vmem],
        out_specs=vmem,
        scratch_shapes=[
            pltpu.VMEM((width, width), jnp.float32),
            pltpu.VMEM((width, width), jnp.bfloat16),
            pltpu.VMEM((width, width), jnp.bfloat16),
            pltpu.VMEM((1, width), jnp.float32),
            pltpu.VMEM((rows, width), jnp.float32),
        ],
        compiler_params=pltpu.CompilerParams(vmem_limit_bytes=24 * 2**20),
        cost_estimate=pl.CostEstimate(flops=4 * width**3, bytes_accessed=6 * rows * width, transcendentals=0),
    )(side, plan, mine, theirs, mine_gram)


def place_own_kernel(side_ref, plan_ref, own_ref, out_ref, whole, sems):
    blocks = out_ref.shape[0]
    pieces = sems.shape[0]
    piece = blocks // pieces
    more, count = plan_ref[MORE, 0], plan_ref[COUNT, 0]
    first = side_ref[0] * more
    copies = []
    for p in range(pieces):
        for block in range(p * piece, (p + 1) * piece):
            rank = plan_ref[RANK, block]
            place = jnp.where(rank < first, rank, rank - more)
            held = (rank < count) & ((rank < first) | (rank >= first + more))
            rows = own_ref[jnp.where(held, place, 0)]
            whole[block] = jnp.where(held, rows, jnp.zeros_like(rows))
        part = pl.ds(p * piece, piece)
        copies.append(pltpu.make_async_copy(whole.at[part], out_ref.at[part], sems.at[p]))
        copies[-1].start()
    for copy in copies:
        copy.wait()


def place_own(side, plan, own):
    blocks = plan.shape[1]
    shape = (blocks,) + own.shape[1:]
    smem = pl.BlockSpec(memory_space=pltpu.SMEM)
    return pl.pallas_call(
        place_own_kernel,
        out_shape=jax.ShapeDtypeStruct(shape, own.dtype),
        in_specs=[smem, smem, pl.BlockSpec(memory_space=pltpu.VMEM)],
        out_specs=pl.BlockSpec(memory_space=pltpu.HBM),
        scratch_shapes=[pltpu.VMEM(shape, own.dtype), pltpu.SemaphoreType.DMA((8,))],
        compiler_params=pltpu.CompilerParams(vmem_limit_bytes=8 * 2**20),
        cost_estimate=pl.CostEstimate(flops=0, bytes_accessed=4 * own.size, transcendentals=0),
    )(side, plan, own)


def place_others_kernel(side_ref, plan_ref, held_ref, *refs):
    parts, out_ref, sems = refs[:-2], refs[-2], refs[-1]
    position = side_ref[0] * sum(part.shape[0] for part in parts)
    for index, part in enumerate(parts):
        for q in range(part.shape[0]):
            target = out_ref.at[plan_ref[BLOCK, position + q]]
            pltpu.make_async_copy(part.at[q], target, sems.at[index]).start()
        position += part.shape[0]
    for index, part in enumerate(parts):
        pltpu.make_async_copy(part, part, sems.at[index]).wait()


def place_others(side, plan, held, parts):
    smem = pl.BlockSpec(memory_space=pltpu.SMEM)
    vmem = pl.BlockSpec(memory_space=pltpu.VMEM)
    hbm = pl.BlockSpec(memory_space=pltpu.HBM)
    size = sum(part.size for part in parts)
    return pl.pallas_call(
        place_others_kernel,
        out_shape=jax.ShapeDtypeStruct(held.shape, held.dtype),
        in_specs=[smem, smem, hbm] + [vmem] * len(parts),
        out_specs=hbm,
        scratch_shapes=[pltpu.SemaphoreType.DMA((len(parts),))],
        input_output_aliases={2: 0},
        compiler_params=pltpu.CompilerParams(vmem_limit_bytes=6 * 2**20),
        cost_estimate=pl.CostEstimate(flops=0, bytes_accessed=4 * size, transcendentals=0),
    )(side, plan, held, *parts)


def exchange(handed, side, plan, own):
    planes = lax.axis_size("x")
    start, parts = 0, []
    for size, step in zip(handed, (1, -1)):
        if size:
            pairs = [(i, (i + step) % planes) for i in range(planes)]
            parts.append(lax.ppermute(own[start : start + size], "x", pairs))
            start += size
    held = place_own(side, plan, own)
    return place_others(side, plan, held, parts) if parts else held


def body(grads, owners, counts):
    blocks, rows_dev, width = grads.shape
    chips = lax.axis_size("yz")
    side = jnp.stack([lax.axis_index("x") % 2, lax.axis_index("yz")]).astype(jnp.int32)

    outgoing, plan, tier = make_plan(side, owners, counts, grads, chips)
    mine = lax.all_to_all(outgoing, "yz", split_axis=0, concat_axis=0, tiled=True)
    mine = mine.reshape(chips * rows_dev, width)
    theirs = lax.ppermute(mine, "c", [(0, 1), (1, 0)])
    done = refresh(side, plan, mine, theirs, gram(mine))
    own = lax.all_to_all(
        done.reshape(chips, rows_dev, width), "yz", split_axis=0, concat_axis=0, tiled=True
    )
    branches = [functools.partial(exchange, handed) for handed in HANDED]
    return lax.switch(tier[0], branches, side, plan, own)


def solution(mesh):
    fine = Mesh(mesh.devices.reshape(64, 2, 4), ("yz", "c", "x"))
    rows = P(None, ("yz", "c"), None)
    return jax.shard_map(body, mesh=fine, in_specs=(rows, P(), P()), out_specs=rows, check_vma=False)
```

```python
import functools

import jax
import jax.numpy as jnp
from jax import lax
from jax.experimental import pallas as pl
from jax.experimental.pallas import tpu as pltpu
from jax.sharding import Mesh
from jax.sharding import PartitionSpec as P

EPS = 1e-06
TILE = 256
HANDED = (
    *((0, 0), (4, 0), (8, 0), (12, 0), (16, 0), (15, 5)),
    *((17, 7), (19, 9), (21, 11), (25, 15), (29, 19), (37, 27)),
)
BLOCK, RANK, TIER, MORE, COUNT = range(5)


def down_columns(row):
    n = row.shape[1]
    return jnp.broadcast_to(row, (n, n)).T


def plan_kernel(
    side_ref, owners_ref, counts_ref, grads_ref, out_ref, plan_ref, tier_ref, whole, rows_ref, plan_sem, whole_sems
):
    piece = whole.shape[0] // whole_sems.shape[0]
    loads = []
    for p in range(whole_sems.shape[0]):
        part = pl.ds(p * piece, piece)
        loads.append(pltpu.make_async_copy(grads_ref.at[part], whole.at[part], whole_sems.at[p]))
        loads[-1].start()
    places, blocks = out_ref.shape[0], owners_ref.shape[1]
    square = (blocks, blocks)
    i = lax.broadcasted_iota(jnp.int32, square, 0)
    j = lax.broadcasted_iota(jnp.int32, square, 1)
    owners = jnp.broadcast_to(owners_ref[...], square)
    same = (down_columns(owners_ref[...]) == owners) & (i < j)
    slot = jnp.sum(jnp.where(same, 1, 0), axis=0, keepdims=True)
    have = jnp.sum(jnp.where(owners == i, down_columns(counts_ref[...]), 0), axis=0, keepdims=True)
    valid = jnp.where(slot < have, 1, 0)
    before = jnp.sum(jnp.where(i < j, down_columns(valid), 0), axis=0, keepdims=True)
    count = jnp.broadcast_to(jnp.sum(valid, axis=1, keepdims=True), (1, blocks))
    rank = jnp.where(slot < have, before, count + j[:1, :] - before)
    block = jnp.sum(jnp.where(down_columns(rank) == j, i, 0), axis=0, keepdims=True)
    tier, more = jnp.zeros_like(count), jnp.zeros_like(count)
    for smaller, larger in zip(HANDED, HANDED[1:]):
        above = count > places + sum(smaller)
        tier = jnp.where(above, tier + 1, tier)
        more = jnp.where(above, sum(larger), more)
    for index, row in ((BLOCK, block), (RANK, rank), (TIER, tier), (MORE, more), (COUNT, count)):
        rows_ref[index : index + 1, :] = row
    to_scalars = pltpu.make_async_copy(rows_ref, plan_ref, plan_sem)
    to_scalars.start()
    to_scalars.wait()
    for load in loads:
        load.wait()
    tier_ref[0] = plan_ref[TIER, 0]
    more = plan_ref[MORE, 0]
    first = side_ref[0] * more
    for place in range(places):
        position = jnp.where(place < first, place, place + more)
        out_ref[place] = whole[plan_ref[BLOCK, position]]


def make_plan(side, owners, counts, grads, places):
    blocks = grads.shape[0]
    vmem = pl.BlockSpec(memory_space=pltpu.VMEM)
    smem = pl.BlockSpec(memory_space=pltpu.SMEM)
    return pl.pallas_call(
        plan_kernel,
        out_shape=(
            pltpu.VMEM((places,) + grads.shape[1:], grads.dtype),
            jax.ShapeDtypeStruct((8, blocks), jnp.int32),
            jax.ShapeDtypeStruct((1,), jnp.int32),
        ),
        in_specs=[smem, vmem, vmem, pl.BlockSpec(memory_space=pltpu.HBM)],
        out_specs=(vmem, smem, smem),
        scratch_shapes=[
            pltpu.VMEM(grads.shape, grads.dtype),
            pltpu.VMEM((8, blocks), jnp.int32),
            pltpu.SemaphoreType.DMA,
            pltpu.SemaphoreType.DMA((8,)),
        ],
        compiler_params=pltpu.CompilerParams(vmem_limit_bytes=8 * 2**20),
    )(
        side,
        *(
            pltpu.with_memory_space_constraint(array, pltpu.HBM)
            for array in (owners.reshape(1, -1), counts.reshape(1, -1), grads)
        ),
    )


def first_dims(a, b):
    return lax.dot_general(a, b, (((0,), (0,)), ((), ())), preferred_element_type=jnp.float32)


def folded_squares(tile):
    squares = tile * tile
    folded = jnp.sum(squares.reshape(tile.shape[0] // 8, 8, tile.shape[1]), axis=0)
    return sum(folded[:, c : c + 128] for c in range(0, tile.shape[1], 128))


def gram_kernel(rows_ref, out_ref, squares_ref):
    width = rows_ref.shape[1]
    for j in range(0, width, TILE):
        out_ref[j:, j : j + TILE] = first_dims(rows_ref[:, j:], rows_ref[:, j : j + TILE])
    squares_ref[...] = folded_squares(rows_ref[...].astype(jnp.float32))


def gram(rows):
    count, width = rows.shape
    vmem = pl.BlockSpec(memory_space=pltpu.VMEM)
    return pl.pallas_call(
        gram_kernel,
        out_shape=(
            jax.ShapeDtypeStruct((width, width), jnp.float32),
            jax.ShapeDtypeStruct((8, 128), jnp.float32),
        ),
        in_specs=[vmem],
        out_specs=(vmem, vmem),
        compiler_params=pltpu.CompilerParams(vmem_limit_bytes=12 * 2**20),
        cost_estimate=pl.CostEstimate(
            flops=2 * count * width**2, bytes_accessed=2 * count * width + 4 * width**2, transcendentals=0
        ),
    )(rows)


def on_diagonal(tile):
    r = lax.broadcasted_iota(jnp.int32, tile.shape, 0)
    c = lax.broadcasted_iota(jnp.int32, tile.shape, 1)
    return r == c


def refresh_kernel(side_ref, plan_ref, tier_ref, mine_ref, theirs_ref, gram_ref, squares_ref, out_ref, *scratch):
    del tier_ref
    root, square, rest, product = scratch
    rows, width = mine_ref.shape
    place, more = side_ref[1], plan_ref[MORE, 0]
    position = jnp.where(place < side_ref[0] * more, place, place + more)
    valid = jnp.where(position < plan_ref[COUNT, 0], 1.0, 0.0)

    total_sq = squares_ref[...] + folded_squares(theirs_ref[...].astype(jnp.float32))
    total_sq = jnp.sum(total_sq, keepdims=True)
    scale_c = total_sq / width + EPS
    quarter = lax.rsqrt(jnp.sqrt(scale_c)) * 0.25
    slope = quarter / scale_c
    diag = 5.0 * quarter - EPS * slope

    for j in range(0, width, TILE):
        cols = slice(j, j + TILE)
        tile = gram_ref[j:, cols] + first_dims(theirs_ref[:, j:], theirs_ref[:, cols])
        tile = -slope * tile
        top = tile[:TILE]
        top = jnp.where(on_diagonal(top), diag + top, top)
        kept = top.astype(jnp.bfloat16)
        root[cols, cols] = kept
        kept = kept.astype(jnp.float32)
        off = jnp.where(on_diagonal(top), 2.0 * (top - kept) * kept, 0.0)
        rest[:, cols] = jnp.sum(off, axis=0, keepdims=True)
        if j + TILE < width:
            below = tile[TILE:].astype(jnp.bfloat16)
            root[j + TILE :, cols] = below
            root[cols, j + TILE :] = below.T

    for j in range(0, width, TILE):
        cols = slice(j, j + TILE)
        tile = jnp.dot(root[j:, :], root[:, cols], preferred_element_type=jnp.float32)
        top = tile[:TILE]
        kept = top.astype(jnp.bfloat16)
        square[cols, cols] = kept
        off = jnp.where(on_diagonal(top), top - kept.astype(jnp.float32), 0.0)
        rest[:, cols] += jnp.sum(off, axis=0, keepdims=True)
        if j + TILE < width:
            below = tile[TILE:].astype(jnp.bfloat16)
            square[j + TILE :, cols] = below
            square[cols, j + TILE :] = below.T

    squares = jnp.zeros((8, 128), jnp.float32)
    for j in range(0, width, TILE):
        cols = slice(j, j + TILE)
        for ref in (mine_ref, theirs_ref):
            done = jnp.dot(ref[...], square[:, cols], preferred_element_type=jnp.float32)
            done = done + ref[:, cols].astype(jnp.float32) * rest[:, cols]
            squares += folded_squares(done)
            if ref is mine_ref:
                product[:, cols] = done
    product_sq = jnp.sum(squares, keepdims=True)
    graft = jnp.sqrt((total_sq + EPS) / (product_sq + EPS)) * valid
    out_ref[...] = (product[...] * graft).astype(jnp.bfloat16)


def refresh(side, plan, tier, mine, theirs, mine_gram, mine_squares):
    rows, width = mine.shape
    vmem = pl.BlockSpec(memory_space=pltpu.VMEM)
    smem = pl.BlockSpec(memory_space=pltpu.SMEM)
    return pl.pallas_call(
        refresh_kernel,
        out_shape=jax.ShapeDtypeStruct((rows, width), jnp.bfloat16),
        in_specs=[smem, smem, smem, vmem, vmem, vmem, vmem],
        out_specs=vmem,
        scratch_shapes=[
            pltpu.VMEM((width, width), jnp.bfloat16),
            pltpu.VMEM((width, width), jnp.bfloat16),
            pltpu.VMEM((1, width), jnp.float32),
            pltpu.VMEM((rows, width), jnp.float32),
        ],
        compiler_params=pltpu.CompilerParams(vmem_limit_bytes=14 * 2**20),
        cost_estimate=pl.CostEstimate(flops=4 * width**3, bytes_accessed=6 * rows * width, transcendentals=0),
    )(side, plan, tier, mine, theirs, mine_gram, mine_squares)


def place_own_kernel(side_ref, plan_ref, own_ref, out_ref, whole, sems):
    blocks = out_ref.shape[0]
    pieces = sems.shape[0]
    piece = blocks // pieces
    more, count = plan_ref[MORE, 0], plan_ref[COUNT, 0]
    first = side_ref[0] * more
    copies = []
    for p in range(pieces):
        for block in range(p * piece, (p + 1) * piece):
            rank = plan_ref[RANK, block]
            place = jnp.where(rank < first, rank, rank - more)
            held = (rank < count) & ((rank < first) | (rank >= first + more))
            rows = own_ref[jnp.where(held, place, 0)]
            whole[block] = jnp.where(held, rows, jnp.zeros_like(rows))
        part = pl.ds(p * piece, piece)
        copies.append(pltpu.make_async_copy(whole.at[part], out_ref.at[part], sems.at[p]))
        copies[-1].start()
    for copy in copies:
        copy.wait()


def place_own(side, plan, own):
    blocks = plan.shape[1]
    shape = (blocks,) + own.shape[1:]
    smem = pl.BlockSpec(memory_space=pltpu.SMEM)
    return pl.pallas_call(
        place_own_kernel,
        out_shape=jax.ShapeDtypeStruct(shape, own.dtype),
        in_specs=[smem, smem, pl.BlockSpec(memory_space=pltpu.VMEM)],
        out_specs=pl.BlockSpec(memory_space=pltpu.HBM),
        scratch_shapes=[pltpu.VMEM(shape, own.dtype), pltpu.SemaphoreType.DMA((8,))],
        compiler_params=pltpu.CompilerParams(vmem_limit_bytes=8 * 2**20),
        cost_estimate=pl.CostEstimate(flops=0, bytes_accessed=4 * own.size, transcendentals=0),
    )(side, plan, own)


def place_others_kernel(side_ref, plan_ref, held_ref, *refs):
    parts, out_ref, sems = refs[:-2], refs[-2], refs[-1]
    position = side_ref[0] * sum(part.shape[0] for part in parts)
    for index, part in enumerate(parts):
        for q in range(part.shape[0]):
            target = out_ref.at[plan_ref[BLOCK, position + q]]
            pltpu.make_async_copy(part.at[q], target, sems.at[index]).start()
        position += part.shape[0]
    for index, part in enumerate(parts):
        pltpu.make_async_copy(part, part, sems.at[index]).wait()


def place_others(side, plan, held, parts):
    smem = pl.BlockSpec(memory_space=pltpu.SMEM)
    vmem = pl.BlockSpec(memory_space=pltpu.VMEM)
    hbm = pl.BlockSpec(memory_space=pltpu.HBM)
    size = sum(part.size for part in parts)
    return pl.pallas_call(
        place_others_kernel,
        out_shape=jax.ShapeDtypeStruct(held.shape, held.dtype),
        in_specs=[smem, smem, hbm] + [vmem] * len(parts),
        out_specs=hbm,
        scratch_shapes=[pltpu.SemaphoreType.DMA((len(parts),))],
        input_output_aliases={2: 0},
        compiler_params=pltpu.CompilerParams(vmem_limit_bytes=6 * 2**20),
        cost_estimate=pl.CostEstimate(flops=0, bytes_accessed=4 * size, transcendentals=0),
    )(side, plan, held, *parts)


def exchange(handed, side, plan, own):
    planes = lax.axis_size("x")
    start, parts = 0, []
    for size, step in zip(handed, (1, -1)):
        if size:
            pairs = [(i, (i + step) % planes) for i in range(planes)]
            parts.append(lax.ppermute(own[start : start + size], "x", pairs))
            start += size
    held = place_own(side, plan, own)
    return place_others(side, plan, held, parts) if parts else held


def body(grads, owners, counts):
    blocks, rows_dev, width = grads.shape
    chips = lax.axis_size("yz")
    side = jnp.stack([lax.axis_index("x") % 2, lax.axis_index("yz")]).astype(jnp.int32)

    outgoing, plan, tier = make_plan(side, owners, counts, grads, chips)
    mine = lax.all_to_all(outgoing, "yz", split_axis=0, concat_axis=0, tiled=True)
    mine = mine.reshape(chips * rows_dev, width)
    theirs = lax.ppermute(mine, "c", [(0, 1), (1, 0)])
    tier = lax.clamp(0, tier[0], len(HANDED) - 1)
    done = refresh(side, plan, tier.reshape(1), mine, theirs, *gram(mine))
    own = lax.all_to_all(
        done.reshape(chips, rows_dev, width), "yz", split_axis=0, concat_axis=0, tiled=True
    )
    branches = [functools.partial(exchange, handed) for handed in HANDED]
    return lax.switch(tier, branches, side, plan, own)


def solution(mesh):
    fine = Mesh(mesh.devices.reshape(64, 2, 4), ("yz", "c", "x"))
    rows = P(None, ("yz", "c"), None)
    return jax.shard_map(body, mesh=fine, in_specs=(rows, P(), P()), out_specs=rows, check_vma=False)
```

```python
import functools

import jax
import jax.numpy as jnp
from jax import lax
from jax.experimental import pallas as pl
from jax.experimental.pallas import tpu as pltpu
from jax.sharding import Mesh
from jax.sharding import PartitionSpec as P

EPS = 1e-06
TILE = 256
HANDED = (0, 4, 8, 12, 16, 20, 24, 28, 32, 40, 48, 64)
BLOCK, RANK, TIER, MORE, COUNT = range(5)


def down_columns(row):
    n = row.shape[1]
    return jnp.broadcast_to(row, (n, n)).T


def plan_kernel(
    side_ref, owners_ref, counts_ref, grads_ref, out_ref, plan_ref, tier_ref, whole, rows_ref, plan_sem, whole_sems
):
    piece = whole.shape[0] // whole_sems.shape[0]
    loads = []
    for p in range(whole_sems.shape[0]):
        part = pl.ds(p * piece, piece)
        loads.append(pltpu.make_async_copy(grads_ref.at[part], whole.at[part], whole_sems.at[p]))
        loads[-1].start()
    places, blocks = out_ref.shape[0], owners_ref.shape[1]
    square = (blocks, blocks)
    i = lax.broadcasted_iota(jnp.int32, square, 0)
    j = lax.broadcasted_iota(jnp.int32, square, 1)
    owners = jnp.broadcast_to(owners_ref[...], square)
    same = (down_columns(owners_ref[...]) == owners) & (i < j)
    slot = jnp.sum(jnp.where(same, 1, 0), axis=0, keepdims=True)
    have = jnp.sum(jnp.where(owners == i, down_columns(counts_ref[...]), 0), axis=0, keepdims=True)
    valid = jnp.where(slot < have, 1, 0)
    before = jnp.sum(jnp.where(i < j, down_columns(valid), 0), axis=0, keepdims=True)
    count = jnp.broadcast_to(jnp.sum(valid, axis=1, keepdims=True), (1, blocks))
    rank = jnp.where(slot < have, before, count + j[:1, :] - before)
    block = jnp.sum(jnp.where(down_columns(rank) == j, i, 0), axis=0, keepdims=True)
    tier, more = jnp.zeros_like(count), jnp.zeros_like(count)
    for smaller, larger in zip(HANDED, HANDED[1:]):
        above = count > places + smaller
        tier = jnp.where(above, tier + 1, tier)
        more = jnp.where(above, larger, more)
    for index, row in ((BLOCK, block), (RANK, rank), (TIER, tier), (MORE, more), (COUNT, count)):
        rows_ref[index : index + 1, :] = row
    to_scalars = pltpu.make_async_copy(rows_ref, plan_ref, plan_sem)
    to_scalars.start()
    to_scalars.wait()
    for load in loads:
        load.wait()
    tier_ref[0] = plan_ref[TIER, 0]
    more = plan_ref[MORE, 0]
    first = side_ref[0] * more
    for place in range(places):
        position = jnp.where(place < first, place, place + more)
        out_ref[place] = whole[plan_ref[BLOCK, position]]


def make_plan(side, owners, counts, grads, places):
    blocks = grads.shape[0]
    vmem = pl.BlockSpec(memory_space=pltpu.VMEM)
    smem = pl.BlockSpec(memory_space=pltpu.SMEM)
    return pl.pallas_call(
        plan_kernel,
        out_shape=(
            pltpu.VMEM((places,) + grads.shape[1:], grads.dtype),
            jax.ShapeDtypeStruct((8, blocks), jnp.int32),
            jax.ShapeDtypeStruct((1,), jnp.int32),
        ),
        in_specs=[smem, vmem, vmem, pl.BlockSpec(memory_space=pltpu.HBM)],
        out_specs=(vmem, smem, smem),
        scratch_shapes=[
            pltpu.VMEM(grads.shape, grads.dtype),
            pltpu.VMEM((8, blocks), jnp.int32),
            pltpu.SemaphoreType.DMA,
            pltpu.SemaphoreType.DMA((8,)),
        ],
        compiler_params=pltpu.CompilerParams(vmem_limit_bytes=8 * 2**20),
    )(
        side,
        *(
            pltpu.with_memory_space_constraint(array, pltpu.HBM)
            for array in (owners.reshape(1, -1), counts.reshape(1, -1), grads)
        ),
    )


def first_dims(a, b):
    return lax.dot_general(a, b, (((0,), (0,)), ((), ())), preferred_element_type=jnp.float32)


def folded_squares(tile):
    squares = tile * tile
    folded = jnp.sum(squares.reshape(tile.shape[0] // 8, 8, tile.shape[1]), axis=0)
    return sum(folded[:, c : c + 128] for c in range(0, tile.shape[1], 128))


def gram_kernel(rows_ref, out_ref, squares_ref):
    width = rows_ref.shape[1]
    for j in range(0, width, TILE):
        out_ref[j:, j : j + TILE] = first_dims(rows_ref[:, j:], rows_ref[:, j : j + TILE])
    squares_ref[...] = folded_squares(rows_ref[...].astype(jnp.float32))


def gram(rows):
    count, width = rows.shape
    vmem = pl.BlockSpec(memory_space=pltpu.VMEM)
    return pl.pallas_call(
        gram_kernel,
        out_shape=(
            jax.ShapeDtypeStruct((width, width), jnp.float32),
            jax.ShapeDtypeStruct((8, 128), jnp.float32),
        ),
        in_specs=[vmem],
        out_specs=(vmem, vmem),
        compiler_params=pltpu.CompilerParams(vmem_limit_bytes=12 * 2**20),
        cost_estimate=pl.CostEstimate(
            flops=2 * count * width**2, bytes_accessed=2 * count * width + 4 * width**2, transcendentals=0
        ),
    )(rows)


def on_diagonal(tile):
    r = lax.broadcasted_iota(jnp.int32, tile.shape, 0)
    c = lax.broadcasted_iota(jnp.int32, tile.shape, 1)
    return r == c


def refresh_kernel(side_ref, plan_ref, tier_ref, mine_ref, theirs_ref, gram_ref, squares_ref, out_ref, *scratch):
    del tier_ref
    root, square, rest, product = scratch
    rows, width = mine_ref.shape
    place, more = side_ref[1], plan_ref[MORE, 0]
    position = jnp.where(place < side_ref[0] * more, place, place + more)
    valid = jnp.where(position < plan_ref[COUNT, 0], 1.0, 0.0)

    total_sq = squares_ref[...] + folded_squares(theirs_ref[...].astype(jnp.float32))
    total_sq = jnp.sum(total_sq, keepdims=True)
    scale_c = total_sq / width + EPS
    quarter = lax.rsqrt(jnp.sqrt(scale_c)) * 0.25
    slope = quarter / scale_c
    diag = 5.0 * quarter - EPS * slope

    for j in range(0, width, TILE):
        cols = slice(j, j + TILE)
        tile = gram_ref[j:, cols] + first_dims(theirs_ref[:, j:], theirs_ref[:, cols])
        tile = -slope * tile
        top = tile[:TILE]
        top = jnp.where(on_diagonal(top), diag + top, top)
        kept = top.astype(jnp.bfloat16)
        root[cols, cols] = kept
        kept = kept.astype(jnp.float32)
        off = jnp.where(on_diagonal(top), 2.0 * (top - kept) * kept, 0.0)
        rest[:, cols] = jnp.sum(off, axis=0, keepdims=True)
        if j + TILE < width:
            below = tile[TILE:].astype(jnp.bfloat16)
            root[j + TILE :, cols] = below
            root[cols, j + TILE :] = below.T

    for j in range(0, width, TILE):
        cols = slice(j, j + TILE)
        tile = jnp.dot(root[j:, :], root[:, cols], preferred_element_type=jnp.float32)
        top = tile[:TILE]
        kept = top.astype(jnp.bfloat16)
        square[cols, cols] = kept
        off = jnp.where(on_diagonal(top), top - kept.astype(jnp.float32), 0.0)
        rest[:, cols] += jnp.sum(off, axis=0, keepdims=True)
        if j + TILE < width:
            below = tile[TILE:].astype(jnp.bfloat16)
            square[j + TILE :, cols] = below
            square[cols, j + TILE :] = below.T

    squares = jnp.zeros((8, 128), jnp.float32)
    for j in range(0, width, TILE):
        cols = slice(j, j + TILE)
        for ref in (mine_ref, theirs_ref):
            done = jnp.dot(ref[...], square[:, cols], preferred_element_type=jnp.float32)
            done = done + ref[:, cols].astype(jnp.float32) * rest[:, cols]
            squares += folded_squares(done)
            if ref is mine_ref:
                product[:, cols] = done
    product_sq = jnp.sum(squares, keepdims=True)
    graft = jnp.sqrt((total_sq + EPS) / (product_sq + EPS)) * valid
    out_ref[...] = (product[...] * graft).astype(jnp.bfloat16)


def refresh(side, plan, tier, mine, theirs, mine_gram, mine_squares):
    rows, width = mine.shape
    vmem = pl.BlockSpec(memory_space=pltpu.VMEM)
    smem = pl.BlockSpec(memory_space=pltpu.SMEM)
    return pl.pallas_call(
        refresh_kernel,
        out_shape=jax.ShapeDtypeStruct((rows, width), jnp.bfloat16),
        in_specs=[smem, smem, smem, vmem, vmem, vmem, vmem],
        out_specs=vmem,
        scratch_shapes=[
            pltpu.VMEM((width, width), jnp.bfloat16),
            pltpu.VMEM((width, width), jnp.bfloat16),
            pltpu.VMEM((1, width), jnp.float32),
            pltpu.VMEM((rows, width), jnp.float32),
        ],
        compiler_params=pltpu.CompilerParams(vmem_limit_bytes=14 * 2**20),
        cost_estimate=pl.CostEstimate(flops=4 * width**3, bytes_accessed=6 * rows * width, transcendentals=0),
    )(side, plan, tier, mine, theirs, mine_gram, mine_squares)


def place_own_kernel(side_ref, plan_ref, own_ref, out_ref, whole, sems):
    blocks = out_ref.shape[0]
    pieces = sems.shape[0]
    piece = blocks // pieces
    more, count = plan_ref[MORE, 0], plan_ref[COUNT, 0]
    first = side_ref[0] * more
    copies = []
    for p in range(pieces):
        for block in range(p * piece, (p + 1) * piece):
            rank = plan_ref[RANK, block]
            place = jnp.where(rank < first, rank, rank - more)
            held = (rank < count) & ((rank < first) | (rank >= first + more))
            rows = own_ref[jnp.where(held, place, 0)]
            whole[block] = jnp.where(held, rows, jnp.zeros_like(rows))
        part = pl.ds(p * piece, piece)
        copies.append(pltpu.make_async_copy(whole.at[part], out_ref.at[part], sems.at[p]))
        copies[-1].start()
    for copy in copies:
        copy.wait()


def place_own(side, plan, own):
    blocks = plan.shape[1]
    shape = (blocks,) + own.shape[1:]
    smem = pl.BlockSpec(memory_space=pltpu.SMEM)
    return pl.pallas_call(
        place_own_kernel,
        out_shape=jax.ShapeDtypeStruct(shape, own.dtype),
        in_specs=[smem, smem, pl.BlockSpec(memory_space=pltpu.VMEM)],
        out_specs=pl.BlockSpec(memory_space=pltpu.HBM),
        scratch_shapes=[pltpu.VMEM(shape, own.dtype), pltpu.SemaphoreType.DMA((8,))],
        compiler_params=pltpu.CompilerParams(vmem_limit_bytes=8 * 2**20),
        cost_estimate=pl.CostEstimate(flops=0, bytes_accessed=4 * own.size, transcendentals=0),
    )(side, plan, own)


def place_others_kernel(side_ref, plan_ref, held_ref, got_ref, out_ref, sem):
    size = got_ref.shape[0]
    first = side_ref[0] * size
    for q in range(size):
        target = out_ref.at[plan_ref[BLOCK, first + q]]
        pltpu.make_async_copy(got_ref.at[q], target, sem).start()
    pltpu.make_async_copy(got_ref, got_ref, sem).wait()


def place_others(side, plan, held, got):
    smem = pl.BlockSpec(memory_space=pltpu.SMEM)
    vmem = pl.BlockSpec(memory_space=pltpu.VMEM)
    hbm = pl.BlockSpec(memory_space=pltpu.HBM)
    return pl.pallas_call(
        place_others_kernel,
        out_shape=jax.ShapeDtypeStruct(held.shape, held.dtype),
        in_specs=[smem, smem, hbm, vmem],
        out_specs=hbm,
        scratch_shapes=[pltpu.SemaphoreType.DMA],
        input_output_aliases={2: 0},
        compiler_params=pltpu.CompilerParams(vmem_limit_bytes=6 * 2**20),
        cost_estimate=pl.CostEstimate(flops=0, bytes_accessed=4 * got.size, transcendentals=0),
    )(side, plan, held, got)


def exchange(handed, side, plan, own):
    if handed == 0:
        return place_own(side, plan, own)
    planes, cores = lax.axis_size("x"), lax.axis_size("c")
    pairs = [
        (core * planes + x, core * planes + (x + 1 - 2 * core) % planes)
        for core in range(cores)
        for x in range(planes)
    ]
    got = lax.ppermute(own[:handed], ("c", "x"), pairs)
    held = place_own(side, plan, own)
    return place_others(side, plan, held, got)


def body(grads, owners, counts):
    blocks, rows_dev, width = grads.shape
    chips = lax.axis_size("yz")
    side = jnp.stack([lax.axis_index("x") % 2, lax.axis_index("yz")]).astype(jnp.int32)

    outgoing, plan, tier = make_plan(side, owners, counts, grads, chips)
    mine = lax.all_to_all(outgoing, "yz", split_axis=0, concat_axis=0, tiled=True)
    mine = mine.reshape(chips * rows_dev, width)
    theirs = lax.ppermute(mine, "c", [(0, 1), (1, 0)])
    tier = lax.clamp(0, tier[0], len(HANDED) - 1)
    done = refresh(side, plan, tier.reshape(1), mine, theirs, *gram(mine))
    own = lax.all_to_all(
        done.reshape(chips, rows_dev, width), "yz", split_axis=0, concat_axis=0, tiled=True
    )
    branches = [functools.partial(exchange, handed) for handed in HANDED]
    return lax.switch(tier, branches, side, plan, own)


def solution(mesh):
    fine = Mesh(mesh.devices.reshape(64, 2, 4), ("yz", "c", "x"))
    rows = P(None, ("yz", "c"), None)
    return jax.shard_map(body, mesh=fine, in_specs=(rows, P(), P()), out_specs=rows, check_vma=False)
```

```python
import functools

import jax
import jax.numpy as jnp
from jax import lax
from jax.experimental import pallas as pl
from jax.experimental.pallas import tpu as pltpu
from jax.sharding import Mesh
from jax.sharding import PartitionSpec as P

EPS = 1e-06
TILE = 256
HANDED = (
    *((0, 0), (4, 0), (8, 0), (12, 0), (16, 0), (20, 0)),
    *((18, 6), (20, 8), (22, 10), (26, 14), (30, 18), (38, 26)),
)
BLOCK, RANK, TIER, MORE, COUNT = range(5)


def down_columns(row):
    n = row.shape[1]
    return jnp.broadcast_to(row, (n, n)).T


def plan_kernel(
    side_ref, owners_ref, counts_ref, grads_ref, out_ref, plan_ref, tier_ref, whole, rows_ref, plan_sem, whole_sems
):
    piece = whole.shape[0] // whole_sems.shape[0]
    loads = []
    for p in range(whole_sems.shape[0]):
        part = pl.ds(p * piece, piece)
        loads.append(pltpu.make_async_copy(grads_ref.at[part], whole.at[part], whole_sems.at[p]))
        loads[-1].start()
    places, blocks = out_ref.shape[0], owners_ref.shape[1]
    square = (blocks, blocks)
    i = lax.broadcasted_iota(jnp.int32, square, 0)
    j = lax.broadcasted_iota(jnp.int32, square, 1)
    owners = jnp.broadcast_to(owners_ref[...], square)
    same = (down_columns(owners_ref[...]) == owners) & (i < j)
    slot = jnp.sum(jnp.where(same, 1, 0), axis=0, keepdims=True)
    have = jnp.sum(jnp.where(owners == i, down_columns(counts_ref[...]), 0), axis=0, keepdims=True)
    valid = jnp.where(slot < have, 1, 0)
    before = jnp.sum(jnp.where(i < j, down_columns(valid), 0), axis=0, keepdims=True)
    count = jnp.broadcast_to(jnp.sum(valid, axis=1, keepdims=True), (1, blocks))
    rank = jnp.where(slot < have, before, count + j[:1, :] - before)
    block = jnp.sum(jnp.where(down_columns(rank) == j, i, 0), axis=0, keepdims=True)
    tier, more = jnp.zeros_like(count), jnp.zeros_like(count)
    for smaller, larger in zip(HANDED, HANDED[1:]):
        above = count > places + sum(smaller)
        tier = jnp.where(above, tier + 1, tier)
        more = jnp.where(above, sum(larger), more)
    for index, row in ((BLOCK, block), (RANK, rank), (TIER, tier), (MORE, more), (COUNT, count)):
        rows_ref[index : index + 1, :] = row
    to_scalars = pltpu.make_async_copy(rows_ref, plan_ref, plan_sem)
    to_scalars.start()
    to_scalars.wait()
    for load in loads:
        load.wait()
    tier_ref[0] = plan_ref[TIER, 0]
    more = plan_ref[MORE, 0]
    first = side_ref[0] * more
    for place in range(places):
        position = jnp.where(place < first, place, place + more)
        out_ref[place] = whole[plan_ref[BLOCK, position]]


def make_plan(side, owners, counts, grads, places):
    blocks = grads.shape[0]
    vmem = pl.BlockSpec(memory_space=pltpu.VMEM)
    smem = pl.BlockSpec(memory_space=pltpu.SMEM)
    return pl.pallas_call(
        plan_kernel,
        out_shape=(
            pltpu.VMEM((places,) + grads.shape[1:], grads.dtype),
            jax.ShapeDtypeStruct((8, blocks), jnp.int32),
            jax.ShapeDtypeStruct((1,), jnp.int32),
        ),
        in_specs=[smem, vmem, vmem, pl.BlockSpec(memory_space=pltpu.HBM)],
        out_specs=(vmem, smem, smem),
        scratch_shapes=[
            pltpu.VMEM(grads.shape, grads.dtype),
            pltpu.VMEM((8, blocks), jnp.int32),
            pltpu.SemaphoreType.DMA,
            pltpu.SemaphoreType.DMA((8,)),
        ],
        compiler_params=pltpu.CompilerParams(vmem_limit_bytes=8 * 2**20),
    )(
        side,
        *(
            pltpu.with_memory_space_constraint(array, pltpu.HBM)
            for array in (owners.reshape(1, -1), counts.reshape(1, -1), grads)
        ),
    )


def first_dims(a, b):
    return lax.dot_general(a, b, (((0,), (0,)), ((), ())), preferred_element_type=jnp.float32)


def folded_squares(tile):
    squares = tile * tile
    folded = jnp.sum(squares.reshape(tile.shape[0] // 8, 8, tile.shape[1]), axis=0)
    return sum(folded[:, c : c + 128] for c in range(0, tile.shape[1], 128))


def gram_kernel(rows_ref, out_ref, squares_ref):
    width = rows_ref.shape[1]
    for j in range(0, width, TILE):
        out_ref[j:, j : j + TILE] = first_dims(rows_ref[:, j:], rows_ref[:, j : j + TILE])
    squares_ref[...] = folded_squares(rows_ref[...].astype(jnp.float32))


def gram(rows):
    count, width = rows.shape
    vmem = pl.BlockSpec(memory_space=pltpu.VMEM)
    return pl.pallas_call(
        gram_kernel,
        out_shape=(
            jax.ShapeDtypeStruct((width, width), jnp.float32),
            jax.ShapeDtypeStruct((8, 128), jnp.float32),
        ),
        in_specs=[vmem],
        out_specs=(vmem, vmem),
        compiler_params=pltpu.CompilerParams(vmem_limit_bytes=12 * 2**20),
        cost_estimate=pl.CostEstimate(
            flops=2 * count * width**2, bytes_accessed=2 * count * width + 4 * width**2, transcendentals=0
        ),
    )(rows)


def on_diagonal(tile):
    r = lax.broadcasted_iota(jnp.int32, tile.shape, 0)
    c = lax.broadcasted_iota(jnp.int32, tile.shape, 1)
    return r == c


def refresh_kernel(side_ref, plan_ref, tier_ref, mine_ref, theirs_ref, gram_ref, squares_ref, out_ref, *scratch):
    del tier_ref
    root, square, rest, product = scratch
    rows, width = mine_ref.shape
    place, more = side_ref[1], plan_ref[MORE, 0]
    position = jnp.where(place < side_ref[0] * more, place, place + more)
    valid = jnp.where(position < plan_ref[COUNT, 0], 1.0, 0.0)

    total_sq = squares_ref[...] + folded_squares(theirs_ref[...].astype(jnp.float32))
    total_sq = jnp.sum(total_sq, keepdims=True)
    scale_c = total_sq / width + EPS
    quarter = lax.rsqrt(jnp.sqrt(scale_c)) * 0.25
    slope = quarter / scale_c
    diag = 5.0 * quarter - EPS * slope

    for j in range(0, width, TILE):
        cols = slice(j, j + TILE)
        tile = gram_ref[j:, cols] + first_dims(theirs_ref[:, j:], theirs_ref[:, cols])
        tile = -slope * tile
        top = tile[:TILE]
        top = jnp.where(on_diagonal(top), diag + top, top)
        kept = top.astype(jnp.bfloat16)
        root[cols, cols] = kept
        kept = kept.astype(jnp.float32)
        off = jnp.where(on_diagonal(top), 2.0 * (top - kept) * kept, 0.0)
        rest[:, cols] = jnp.sum(off, axis=0, keepdims=True)
        if j + TILE < width:
            below = tile[TILE:].astype(jnp.bfloat16)
            root[j + TILE :, cols] = below
            root[cols, j + TILE :] = below.T

    for j in range(0, width, TILE):
        cols = slice(j, j + TILE)
        tile = jnp.dot(root[j:, :], root[:, cols], preferred_element_type=jnp.float32)
        top = tile[:TILE]
        kept = top.astype(jnp.bfloat16)
        square[cols, cols] = kept
        off = jnp.where(on_diagonal(top), top - kept.astype(jnp.float32), 0.0)
        rest[:, cols] += jnp.sum(off, axis=0, keepdims=True)
        if j + TILE < width:
            below = tile[TILE:].astype(jnp.bfloat16)
            square[j + TILE :, cols] = below
            square[cols, j + TILE :] = below.T

    squares = jnp.zeros((8, 128), jnp.float32)
    for j in range(0, width, TILE):
        cols = slice(j, j + TILE)
        for ref in (mine_ref, theirs_ref):
            done = jnp.dot(ref[...], square[:, cols], preferred_element_type=jnp.float32)
            done = done + ref[:, cols].astype(jnp.float32) * rest[:, cols]
            squares += folded_squares(done)
            if ref is mine_ref:
                product[:, cols] = done
    product_sq = jnp.sum(squares, keepdims=True)
    graft = jnp.sqrt((total_sq + EPS) / (product_sq + EPS)) * valid
    out_ref[...] = (product[...] * graft).astype(jnp.bfloat16)


def refresh(side, plan, tier, mine, theirs, mine_gram, mine_squares):
    rows, width = mine.shape
    vmem = pl.BlockSpec(memory_space=pltpu.VMEM)
    smem = pl.BlockSpec(memory_space=pltpu.SMEM)
    return pl.pallas_call(
        refresh_kernel,
        out_shape=jax.ShapeDtypeStruct((rows, width), jnp.bfloat16),
        in_specs=[smem, smem, smem, vmem, vmem, vmem, vmem],
        out_specs=vmem,
        scratch_shapes=[
            pltpu.VMEM((width, width), jnp.bfloat16),
            pltpu.VMEM((width, width), jnp.bfloat16),
            pltpu.VMEM((1, width), jnp.float32),
            pltpu.VMEM((rows, width), jnp.float32),
        ],
        compiler_params=pltpu.CompilerParams(vmem_limit_bytes=14 * 2**20),
        cost_estimate=pl.CostEstimate(flops=4 * width**3, bytes_accessed=6 * rows * width, transcendentals=0),
    )(side, plan, tier, mine, theirs, mine_gram, mine_squares)


def place_own_kernel(side_ref, plan_ref, own_ref, out_ref, whole, sems):
    blocks = out_ref.shape[0]
    pieces = sems.shape[0]
    piece = blocks // pieces
    more, count = plan_ref[MORE, 0], plan_ref[COUNT, 0]
    first = side_ref[0] * more
    copies = []
    for p in range(pieces):
        for block in range(p * piece, (p + 1) * piece):
            rank = plan_ref[RANK, block]
            place = jnp.where(rank < first, rank, rank - more)
            held = (rank < count) & ((rank < first) | (rank >= first + more))
            rows = own_ref[jnp.where(held, place, 0)]
            whole[block] = jnp.where(held, rows, jnp.zeros_like(rows))
        part = pl.ds(p * piece, piece)
        copies.append(pltpu.make_async_copy(whole.at[part], out_ref.at[part], sems.at[p]))
        copies[-1].start()
    for copy in copies:
        copy.wait()


def place_own(side, plan, own):
    blocks = plan.shape[1]
    shape = (blocks,) + own.shape[1:]
    smem = pl.BlockSpec(memory_space=pltpu.SMEM)
    return pl.pallas_call(
        place_own_kernel,
        out_shape=jax.ShapeDtypeStruct(shape, own.dtype),
        in_specs=[smem, smem, pl.BlockSpec(memory_space=pltpu.VMEM)],
        out_specs=pl.BlockSpec(memory_space=pltpu.HBM),
        scratch_shapes=[pltpu.VMEM(shape, own.dtype), pltpu.SemaphoreType.DMA((8,))],
        compiler_params=pltpu.CompilerParams(vmem_limit_bytes=8 * 2**20),
        cost_estimate=pl.CostEstimate(flops=0, bytes_accessed=4 * own.size, transcendentals=0),
    )(side, plan, own)


def place_others_kernel(side_ref, plan_ref, held_ref, *refs):
    parts, out_ref, sems = refs[:-2], refs[-2], refs[-1]
    position = side_ref[0] * sum(part.shape[0] for part in parts)
    for index, part in enumerate(parts):
        for q in range(part.shape[0]):
            target = out_ref.at[plan_ref[BLOCK, position + q]]
            pltpu.make_async_copy(part.at[q], target, sems.at[index]).start()
        position += part.shape[0]
    for index, part in enumerate(parts):
        pltpu.make_async_copy(part, part, sems.at[index]).wait()


def place_others(side, plan, held, parts):
    smem = pl.BlockSpec(memory_space=pltpu.SMEM)
    vmem = pl.BlockSpec(memory_space=pltpu.VMEM)
    hbm = pl.BlockSpec(memory_space=pltpu.HBM)
    size = sum(part.size for part in parts)
    return pl.pallas_call(
        place_others_kernel,
        out_shape=jax.ShapeDtypeStruct(held.shape, held.dtype),
        in_specs=[smem, smem, hbm] + [vmem] * len(parts),
        out_specs=hbm,
        scratch_shapes=[pltpu.SemaphoreType.DMA((len(parts),))],
        input_output_aliases={2: 0},
        compiler_params=pltpu.CompilerParams(vmem_limit_bytes=6 * 2**20),
        cost_estimate=pl.CostEstimate(flops=0, bytes_accessed=4 * size, transcendentals=0),
    )(side, plan, held, *parts)


def exchange(handed, side, plan, own):
    planes, cores = lax.axis_size("x"), lax.axis_size("c")
    start, parts = 0, []
    for size, steps in zip(handed, ((1, -1), (-1, 1))):
        if size:
            pairs = [
                (core * planes + x, core * planes + (x + steps[core]) % planes)
                for core in range(cores)
                for x in range(planes)
            ]
            parts.append(lax.ppermute(own[start : start + size], ("c", "x"), pairs))
            start += size
    held = place_own(side, plan, own)
    return place_others(side, plan, held, parts) if parts else held


def body(grads, owners, counts):
    blocks, rows_dev, width = grads.shape
    chips = lax.axis_size("yz")
    side = jnp.stack([lax.axis_index("x") % 2, lax.axis_index("yz")]).astype(jnp.int32)

    outgoing, plan, tier = make_plan(side, owners, counts, grads, chips)
    mine = lax.all_to_all(outgoing, "yz", split_axis=0, concat_axis=0, tiled=True)
    mine = mine.reshape(chips * rows_dev, width)
    theirs = lax.ppermute(mine, "c", [(0, 1), (1, 0)])
    tier = lax.clamp(0, tier[0], len(HANDED) - 1)
    done = refresh(side, plan, tier.reshape(1), mine, theirs, *gram(mine))
    own = lax.all_to_all(
        done.reshape(chips, rows_dev, width), "yz", split_axis=0, concat_axis=0, tiled=True
    )
    branches = [functools.partial(exchange, handed) for handed in HANDED]
    return lax.switch(tier, branches, side, plan, own)


def solution(mesh):
    fine = Mesh(mesh.devices.reshape(64, 2, 4), ("yz", "c", "x"))
    rows = P(None, ("yz", "c"), None)
    return jax.shard_map(body, mesh=fine, in_specs=(rows, P(), P()), out_specs=rows, check_vma=False)
```

```python
import functools

import jax
import jax.numpy as jnp
from jax import lax
from jax.experimental import pallas as pl
from jax.experimental.pallas import tpu as pltpu
from jax.sharding import Mesh
from jax.sharding import PartitionSpec as P

EPS = 1e-06
TILE = 256
HANDED = (
    *((size, 0) for size in (0, 4, 8, 10, 12, 14, 16, 18, 20, 22, 24)),
    *((19, 9), (21, 11), (25, 15), (29, 19), (37, 27)),
)
BLOCK, RANK, TIER, MORE, COUNT = range(5)


def down_columns(row):
    n = row.shape[1]
    return jnp.broadcast_to(row, (n, n)).T


def plan_kernel(
    side_ref, owners_ref, counts_ref, grads_ref, out_ref, plan_ref, tier_ref, whole, rows_ref, plan_sem, whole_sems
):
    piece = whole.shape[0] // whole_sems.shape[0]
    loads = []
    for p in range(whole_sems.shape[0]):
        part = pl.ds(p * piece, piece)
        loads.append(pltpu.make_async_copy(grads_ref.at[part], whole.at[part], whole_sems.at[p]))
        loads[-1].start()
    places, blocks = out_ref.shape[0], owners_ref.shape[1]
    square = (blocks, blocks)
    i = lax.broadcasted_iota(jnp.int32, square, 0)
    j = lax.broadcasted_iota(jnp.int32, square, 1)
    owners = jnp.broadcast_to(owners_ref[...], square)
    same = (down_columns(owners_ref[...]) == owners) & (i < j)
    slot = jnp.sum(jnp.where(same, 1, 0), axis=0, keepdims=True)
    have = jnp.sum(jnp.where(owners == i, down_columns(counts_ref[...]), 0), axis=0, keepdims=True)
    valid = jnp.where(slot < have, 1, 0)
    before = jnp.sum(jnp.where(i < j, down_columns(valid), 0), axis=0, keepdims=True)
    count = jnp.broadcast_to(jnp.sum(valid, axis=1, keepdims=True), (1, blocks))
    rank = jnp.where(slot < have, before, count + j[:1, :] - before)
    block = jnp.sum(jnp.where(down_columns(rank) == j, i, 0), axis=0, keepdims=True)
    tier, more = jnp.zeros_like(count), jnp.zeros_like(count)
    for smaller, larger in zip(HANDED, HANDED[1:]):
        above = count > places + sum(smaller)
        tier = jnp.where(above, tier + 1, tier)
        more = jnp.where(above, sum(larger), more)
    for index, row in ((BLOCK, block), (RANK, rank), (TIER, tier), (MORE, more), (COUNT, count)):
        rows_ref[index : index + 1, :] = row
    to_scalars = pltpu.make_async_copy(rows_ref, plan_ref, plan_sem)
    to_scalars.start()
    to_scalars.wait()
    for load in loads:
        load.wait()
    tier_ref[0] = plan_ref[TIER, 0]
    more = plan_ref[MORE, 0]
    first = side_ref[0] * more
    for place in range(places):
        position = jnp.where(place < first, place, place + more)
        out_ref[place] = whole[plan_ref[BLOCK, position]]


def make_plan(side, owners, counts, grads, places):
    blocks = grads.shape[0]
    vmem = pl.BlockSpec(memory_space=pltpu.VMEM)
    smem = pl.BlockSpec(memory_space=pltpu.SMEM)
    return pl.pallas_call(
        plan_kernel,
        out_shape=(
            pltpu.VMEM((places,) + grads.shape[1:], grads.dtype),
            jax.ShapeDtypeStruct((8, blocks), jnp.int32),
            jax.ShapeDtypeStruct((1,), jnp.int32),
        ),
        in_specs=[smem, vmem, vmem, pl.BlockSpec(memory_space=pltpu.HBM)],
        out_specs=(vmem, smem, smem),
        scratch_shapes=[
            pltpu.VMEM(grads.shape, grads.dtype),
            pltpu.VMEM((8, blocks), jnp.int32),
            pltpu.SemaphoreType.DMA,
            pltpu.SemaphoreType.DMA((8,)),
        ],
        compiler_params=pltpu.CompilerParams(vmem_limit_bytes=8 * 2**20),
    )(
        side,
        *(
            pltpu.with_memory_space_constraint(array, pltpu.HBM)
            for array in (owners.reshape(1, -1), counts.reshape(1, -1), grads)
        ),
    )


def first_dims(a, b):
    return lax.dot_general(a, b, (((0,), (0,)), ((), ())), preferred_element_type=jnp.float32)


def folded_squares(tile):
    squares = tile * tile
    folded = jnp.sum(squares.reshape(tile.shape[0] // 8, 8, tile.shape[1]), axis=0)
    return sum(folded[:, c : c + 128] for c in range(0, tile.shape[1], 128))


def gram_kernel(rows_ref, out_ref, squares_ref):
    width = rows_ref.shape[1]
    for j in range(0, width, TILE):
        out_ref[j:, j : j + TILE] = first_dims(rows_ref[:, j:], rows_ref[:, j : j + TILE])
    squares_ref[...] = folded_squares(rows_ref[...].astype(jnp.float32))


def gram(rows):
    count, width = rows.shape
    vmem = pl.BlockSpec(memory_space=pltpu.VMEM)
    return pl.pallas_call(
        gram_kernel,
        out_shape=(
            jax.ShapeDtypeStruct((width, width), jnp.float32),
            jax.ShapeDtypeStruct((8, 128), jnp.float32),
        ),
        in_specs=[vmem],
        out_specs=(vmem, vmem),
        compiler_params=pltpu.CompilerParams(vmem_limit_bytes=12 * 2**20),
        cost_estimate=pl.CostEstimate(
            flops=2 * count * width**2, bytes_accessed=2 * count * width + 4 * width**2, transcendentals=0
        ),
    )(rows)


def on_diagonal(tile):
    r = lax.broadcasted_iota(jnp.int32, tile.shape, 0)
    c = lax.broadcasted_iota(jnp.int32, tile.shape, 1)
    return r == c


def refresh_kernel(side_ref, plan_ref, tier_ref, mine_ref, theirs_ref, gram_ref, squares_ref, out_ref, *scratch):
    del tier_ref
    root, square, rest, product = scratch
    rows, width = mine_ref.shape
    place, more = side_ref[1], plan_ref[MORE, 0]
    position = jnp.where(place < side_ref[0] * more, place, place + more)
    valid = jnp.where(position < plan_ref[COUNT, 0], 1.0, 0.0)

    total_sq = squares_ref[...] + folded_squares(theirs_ref[...].astype(jnp.float32))
    total_sq = jnp.sum(total_sq, keepdims=True)
    scale_c = total_sq / width + EPS
    quarter = lax.rsqrt(jnp.sqrt(scale_c)) * 0.25
    slope = quarter / scale_c
    diag = 5.0 * quarter - EPS * slope

    for j in range(0, width, TILE):
        cols = slice(j, j + TILE)
        tile = gram_ref[j:, cols] + first_dims(theirs_ref[:, j:], theirs_ref[:, cols])
        tile = -slope * tile
        top = tile[:TILE]
        top = jnp.where(on_diagonal(top), diag + top, top)
        kept = top.astype(jnp.bfloat16)
        root[cols, cols] = kept
        kept = kept.astype(jnp.float32)
        off = jnp.where(on_diagonal(top), 2.0 * (top - kept) * kept, 0.0)
        rest[:, cols] = jnp.sum(off, axis=0, keepdims=True)
        if j + TILE < width:
            below = tile[TILE:].astype(jnp.bfloat16)
            root[j + TILE :, cols] = below
            root[cols, j + TILE :] = below.T

    for j in range(0, width, TILE):
        cols = slice(j, j + TILE)
        tile = jnp.dot(root[j:, :], root[:, cols], preferred_element_type=jnp.float32)
        top = tile[:TILE]
        kept = top.astype(jnp.bfloat16)
        square[cols, cols] = kept
        off = jnp.where(on_diagonal(top), top - kept.astype(jnp.float32), 0.0)
        rest[:, cols] += jnp.sum(off, axis=0, keepdims=True)
        if j + TILE < width:
            below = tile[TILE:].astype(jnp.bfloat16)
            square[j + TILE :, cols] = below
            square[cols, j + TILE :] = below.T

    squares = jnp.zeros((8, 128), jnp.float32)
    for j in range(0, width, TILE):
        cols = slice(j, j + TILE)
        for ref in (mine_ref, theirs_ref):
            done = jnp.dot(ref[...], square[:, cols], preferred_element_type=jnp.float32)
            done = done + ref[:, cols].astype(jnp.float32) * rest[:, cols]
            squares += folded_squares(done)
            if ref is mine_ref:
                product[:, cols] = done
    product_sq = jnp.sum(squares, keepdims=True)
    graft = jnp.sqrt((total_sq + EPS) / (product_sq + EPS)) * valid
    out_ref[...] = (product[...] * graft).astype(jnp.bfloat16)


def refresh(side, plan, tier, mine, theirs, mine_gram, mine_squares):
    rows, width = mine.shape
    vmem = pl.BlockSpec(memory_space=pltpu.VMEM)
    smem = pl.BlockSpec(memory_space=pltpu.SMEM)
    return pl.pallas_call(
        refresh_kernel,
        out_shape=jax.ShapeDtypeStruct((rows, width), jnp.bfloat16),
        in_specs=[smem, smem, smem, vmem, vmem, vmem, vmem],
        out_specs=vmem,
        scratch_shapes=[
            pltpu.VMEM((width, width), jnp.bfloat16),
            pltpu.VMEM((width, width), jnp.bfloat16),
            pltpu.VMEM((1, width), jnp.float32),
            pltpu.VMEM((rows, width), jnp.float32),
        ],
        compiler_params=pltpu.CompilerParams(vmem_limit_bytes=14 * 2**20),
        cost_estimate=pl.CostEstimate(flops=4 * width**3, bytes_accessed=6 * rows * width, transcendentals=0),
    )(side, plan, tier, mine, theirs, mine_gram, mine_squares)


def place_own_kernel(side_ref, plan_ref, own_ref, out_ref, whole, sems):
    blocks = out_ref.shape[0]
    pieces = sems.shape[0]
    piece = blocks // pieces
    more, count = plan_ref[MORE, 0], plan_ref[COUNT, 0]
    first = side_ref[0] * more
    copies = []
    for p in range(pieces):
        for block in range(p * piece, (p + 1) * piece):
            rank = plan_ref[RANK, block]
            place = jnp.where(rank < first, rank, rank - more)
            held = (rank < count) & ((rank < first) | (rank >= first + more))
            rows = own_ref[jnp.where(held, place, 0)]
            whole[block] = jnp.where(held, rows, jnp.zeros_like(rows))
        part = pl.ds(p * piece, piece)
        copies.append(pltpu.make_async_copy(whole.at[part], out_ref.at[part], sems.at[p]))
        copies[-1].start()
    for copy in copies:
        copy.wait()


def place_own(side, plan, own):
    blocks = plan.shape[1]
    shape = (blocks,) + own.shape[1:]
    smem = pl.BlockSpec(memory_space=pltpu.SMEM)
    return pl.pallas_call(
        place_own_kernel,
        out_shape=jax.ShapeDtypeStruct(shape, own.dtype),
        in_specs=[smem, smem, pl.BlockSpec(memory_space=pltpu.VMEM)],
        out_specs=pl.BlockSpec(memory_space=pltpu.HBM),
        scratch_shapes=[pltpu.VMEM(shape, own.dtype), pltpu.SemaphoreType.DMA((8,))],
        compiler_params=pltpu.CompilerParams(vmem_limit_bytes=8 * 2**20),
        cost_estimate=pl.CostEstimate(flops=0, bytes_accessed=4 * own.size, transcendentals=0),
    )(side, plan, own)


def place_others_kernel(side_ref, plan_ref, held_ref, *refs):
    parts, out_ref, sems = refs[:-2], refs[-2], refs[-1]
    position = side_ref[0] * sum(part.shape[0] for part in parts)
    for index, part in enumerate(parts):
        for q in range(part.shape[0]):
            target = out_ref.at[plan_ref[BLOCK, position + q]]
            pltpu.make_async_copy(part.at[q], target, sems.at[index]).start()
        position += part.shape[0]
    for index, part in enumerate(parts):
        pltpu.make_async_copy(part, part, sems.at[index]).wait()


def place_others(side, plan, held, parts):
    smem = pl.BlockSpec(memory_space=pltpu.SMEM)
    vmem = pl.BlockSpec(memory_space=pltpu.VMEM)
    hbm = pl.BlockSpec(memory_space=pltpu.HBM)
    size = sum(part.size for part in parts)
    return pl.pallas_call(
        place_others_kernel,
        out_shape=jax.ShapeDtypeStruct(held.shape, held.dtype),
        in_specs=[smem, smem, hbm] + [vmem] * len(parts),
        out_specs=hbm,
        scratch_shapes=[pltpu.SemaphoreType.DMA((len(parts),))],
        input_output_aliases={2: 0},
        compiler_params=pltpu.CompilerParams(vmem_limit_bytes=6 * 2**20),
        cost_estimate=pl.CostEstimate(flops=0, bytes_accessed=4 * size, transcendentals=0),
    )(side, plan, held, *parts)


def exchange(handed, side, plan, own):
    planes, cores = lax.axis_size("x"), lax.axis_size("c")
    steps = ((1, 1), (-1, -1)) if handed[1] else ((1, -1), (0, 0))
    start, parts = 0, []
    for size, step in zip(handed, steps):
        if size:
            pairs = [
                (core * planes + x, core * planes + (x + step[core]) % planes)
                for core in range(cores)
                for x in range(planes)
            ]
            parts.append(lax.ppermute(own[start : start + size], ("c", "x"), pairs))
            start += size
    held = place_own(side, plan, own)
    return place_others(side, plan, held, parts) if parts else held


def body(grads, owners, counts):
    blocks, rows_dev, width = grads.shape
    chips = lax.axis_size("yz")
    side = jnp.stack([lax.axis_index("x") % 2, lax.axis_index("yz")]).astype(jnp.int32)

    outgoing, plan, tier = make_plan(side, owners, counts, grads, chips)
    mine = lax.all_to_all(outgoing, "yz", split_axis=0, concat_axis=0, tiled=True)
    mine = mine.reshape(chips * rows_dev, width)
    theirs = lax.ppermute(mine, "c", [(0, 1), (1, 0)])
    tier = lax.clamp(0, tier[0], len(HANDED) - 1)
    done = refresh(side, plan, tier.reshape(1), mine, theirs, *gram(mine))
    own = lax.all_to_all(
        done.reshape(chips, rows_dev, width), "yz", split_axis=0, concat_axis=0, tiled=True
    )
    branches = [functools.partial(exchange, handed) for handed in HANDED]
    return lax.switch(tier, branches, side, plan, own)


def solution(mesh):
    fine = Mesh(mesh.devices.reshape(64, 2, 4), ("yz", "c", "x"))
    rows = P(None, ("yz", "c"), None)
    return jax.shard_map(body, mesh=fine, in_specs=(rows, P(), P()), out_specs=rows, check_vma=False)
```

```python
import functools

import jax
import jax.numpy as jnp
from jax import lax
from jax.experimental import pallas as pl
from jax.experimental.pallas import tpu as pltpu
from jax.sharding import Mesh
from jax.sharding import PartitionSpec as P

EPS = 1e-06
TILE = 256
HANDED = (
    *((size, 0) for size in (0, 4, 8, 10, 12, 14, 16, 18, 20)),
    *((16, 6), (17, 7), (19, 9), (21, 11), (25, 15), (29, 19), (37, 27)),
)
BLOCK, RANK, TIER, MORE, COUNT = range(5)


def down_columns(row):
    n = row.shape[1]
    return jnp.broadcast_to(row, (n, n)).T


def plan_kernel(
    side_ref, owners_ref, counts_ref, grads_ref, out_ref, plan_ref, tier_ref, whole, rows_ref, plan_sem, whole_sems
):
    piece = whole.shape[0] // whole_sems.shape[0]
    loads = []
    for p in range(whole_sems.shape[0]):
        part = pl.ds(p * piece, piece)
        loads.append(pltpu.make_async_copy(grads_ref.at[part], whole.at[part], whole_sems.at[p]))
        loads[-1].start()
    places, blocks = out_ref.shape[0], owners_ref.shape[1]
    square = (blocks, blocks)
    i = lax.broadcasted_iota(jnp.int32, square, 0)
    j = lax.broadcasted_iota(jnp.int32, square, 1)
    owners = jnp.broadcast_to(owners_ref[...], square)
    same = (down_columns(owners_ref[...]) == owners) & (i < j)
    slot = jnp.sum(jnp.where(same, 1, 0), axis=0, keepdims=True)
    have = jnp.sum(jnp.where(owners == i, down_columns(counts_ref[...]), 0), axis=0, keepdims=True)
    valid = jnp.where(slot < have, 1, 0)
    before = jnp.sum(jnp.where(i < j, down_columns(valid), 0), axis=0, keepdims=True)
    count = jnp.broadcast_to(jnp.sum(valid, axis=1, keepdims=True), (1, blocks))
    rank = jnp.where(slot < have, before, count + j[:1, :] - before)
    block = jnp.sum(jnp.where(down_columns(rank) == j, i, 0), axis=0, keepdims=True)
    tier, more = jnp.zeros_like(count), jnp.zeros_like(count)
    for smaller, larger in zip(HANDED, HANDED[1:]):
        above = count > places + sum(smaller)
        tier = jnp.where(above, tier + 1, tier)
        more = jnp.where(above, sum(larger), more)
    for index, row in ((BLOCK, block), (RANK, rank), (TIER, tier), (MORE, more), (COUNT, count)):
        rows_ref[index : index + 1, :] = row
    to_scalars = pltpu.make_async_copy(rows_ref, plan_ref, plan_sem)
    to_scalars.start()
    to_scalars.wait()
    for load in loads:
        load.wait()
    tier_ref[0] = plan_ref[TIER, 0]
    more = plan_ref[MORE, 0]
    first = side_ref[0] * more
    for place in range(places):
        position = jnp.where(place < first, place, place + more)
        out_ref[place] = whole[plan_ref[BLOCK, position]]


def make_plan(side, owners, counts, grads, places):
    blocks = grads.shape[0]
    vmem = pl.BlockSpec(memory_space=pltpu.VMEM)
    smem = pl.BlockSpec(memory_space=pltpu.SMEM)
    return pl.pallas_call(
        plan_kernel,
        out_shape=(
            pltpu.VMEM((places,) + grads.shape[1:], grads.dtype),
            jax.ShapeDtypeStruct((8, blocks), jnp.int32),
            jax.ShapeDtypeStruct((1,), jnp.int32),
        ),
        in_specs=[smem, vmem, vmem, pl.BlockSpec(memory_space=pltpu.HBM)],
        out_specs=(vmem, smem, smem),
        scratch_shapes=[
            pltpu.VMEM(grads.shape, grads.dtype),
            pltpu.VMEM((8, blocks), jnp.int32),
            pltpu.SemaphoreType.DMA,
            pltpu.SemaphoreType.DMA((8,)),
        ],
        compiler_params=pltpu.CompilerParams(vmem_limit_bytes=8 * 2**20),
    )(
        side,
        *(
            pltpu.with_memory_space_constraint(array, pltpu.HBM)
            for array in (owners.reshape(1, -1), counts.reshape(1, -1), grads)
        ),
    )


def first_dims(a, b):
    return lax.dot_general(a, b, (((0,), (0,)), ((), ())), preferred_element_type=jnp.float32)


def folded_squares(tile):
    squares = tile * tile
    folded = jnp.sum(squares.reshape(tile.shape[0] // 8, 8, tile.shape[1]), axis=0)
    return sum(folded[:, c : c + 128] for c in range(0, tile.shape[1], 128))


def gram_kernel(rows_ref, out_ref, squares_ref):
    width = rows_ref.shape[1]
    for j in range(0, width, TILE):
        out_ref[j:, j : j + TILE] = first_dims(rows_ref[:, j:], rows_ref[:, j : j + TILE])
    squares_ref[...] = folded_squares(rows_ref[...].astype(jnp.float32))


def gram(rows):
    count, width = rows.shape
    vmem = pl.BlockSpec(memory_space=pltpu.VMEM)
    return pl.pallas_call(
        gram_kernel,
        out_shape=(
            jax.ShapeDtypeStruct((width, width), jnp.float32),
            jax.ShapeDtypeStruct((8, 128), jnp.float32),
        ),
        in_specs=[vmem],
        out_specs=(vmem, vmem),
        compiler_params=pltpu.CompilerParams(vmem_limit_bytes=12 * 2**20),
        cost_estimate=pl.CostEstimate(
            flops=2 * count * width**2, bytes_accessed=2 * count * width + 4 * width**2, transcendentals=0
        ),
    )(rows)


def on_diagonal(tile):
    r = lax.broadcasted_iota(jnp.int32, tile.shape, 0)
    c = lax.broadcasted_iota(jnp.int32, tile.shape, 1)
    return r == c


def refresh_kernel(side_ref, plan_ref, tier_ref, mine_ref, theirs_ref, gram_ref, squares_ref, out_ref, *scratch):
    del tier_ref
    root, square, rest, product = scratch
    rows, width = mine_ref.shape
    place, more = side_ref[1], plan_ref[MORE, 0]
    position = jnp.where(place < side_ref[0] * more, place, place + more)
    valid = jnp.where(position < plan_ref[COUNT, 0], 1.0, 0.0)

    total_sq = squares_ref[...] + folded_squares(theirs_ref[...].astype(jnp.float32))
    total_sq = jnp.sum(total_sq, keepdims=True)
    scale_c = total_sq / width + EPS
    quarter = lax.rsqrt(jnp.sqrt(scale_c)) * 0.25
    slope = quarter / scale_c
    diag = 5.0 * quarter - EPS * slope

    for j in range(0, width, TILE):
        cols = slice(j, j + TILE)
        tile = gram_ref[j:, cols] + first_dims(theirs_ref[:, j:], theirs_ref[:, cols])
        tile = -slope * tile
        top = tile[:TILE]
        top = jnp.where(on_diagonal(top), diag + top, top)
        kept = top.astype(jnp.bfloat16)
        root[cols, cols] = kept
        kept = kept.astype(jnp.float32)
        off = jnp.where(on_diagonal(top), 2.0 * (top - kept) * kept, 0.0)
        rest[:, cols] = jnp.sum(off, axis=0, keepdims=True)
        if j + TILE < width:
            below = tile[TILE:].astype(jnp.bfloat16)
            root[j + TILE :, cols] = below
            root[cols, j + TILE :] = below.T

    for j in range(0, width, TILE):
        cols = slice(j, j + TILE)
        tile = jnp.dot(root[j:, :], root[:, cols], preferred_element_type=jnp.float32)
        top = tile[:TILE]
        kept = top.astype(jnp.bfloat16)
        square[cols, cols] = kept
        off = jnp.where(on_diagonal(top), top - kept.astype(jnp.float32), 0.0)
        rest[:, cols] += jnp.sum(off, axis=0, keepdims=True)
        if j + TILE < width:
            below = tile[TILE:].astype(jnp.bfloat16)
            square[j + TILE :, cols] = below
            square[cols, j + TILE :] = below.T

    squares = jnp.zeros((8, 128), jnp.float32)
    for j in range(0, width, TILE):
        cols = slice(j, j + TILE)
        for ref in (mine_ref, theirs_ref):
            done = jnp.dot(ref[...], square[:, cols], preferred_element_type=jnp.float32)
            done = done + ref[:, cols].astype(jnp.float32) * rest[:, cols]
            squares += folded_squares(done)
            if ref is mine_ref:
                product[:, cols] = done
    product_sq = jnp.sum(squares, keepdims=True)
    graft = jnp.sqrt((total_sq + EPS) / (product_sq + EPS)) * valid
    out_ref[...] = (product[...] * graft).astype(jnp.bfloat16)


def refresh(side, plan, tier, mine, theirs, mine_gram, mine_squares):
    rows, width = mine.shape
    vmem = pl.BlockSpec(memory_space=pltpu.VMEM)
    smem = pl.BlockSpec(memory_space=pltpu.SMEM)
    return pl.pallas_call(
        refresh_kernel,
        out_shape=jax.ShapeDtypeStruct((rows, width), jnp.bfloat16),
        in_specs=[smem, smem, smem, vmem, vmem, vmem, vmem],
        out_specs=vmem,
        scratch_shapes=[
            pltpu.VMEM((width, width), jnp.bfloat16),
            pltpu.VMEM((width, width), jnp.bfloat16),
            pltpu.VMEM((1, width), jnp.float32),
            pltpu.VMEM((rows, width), jnp.float32),
        ],
        compiler_params=pltpu.CompilerParams(vmem_limit_bytes=14 * 2**20),
        cost_estimate=pl.CostEstimate(flops=4 * width**3, bytes_accessed=6 * rows * width, transcendentals=0),
    )(side, plan, tier, mine, theirs, mine_gram, mine_squares)


def place_own_kernel(side_ref, plan_ref, own_ref, out_ref, whole, sems):
    blocks = out_ref.shape[0]
    pieces = sems.shape[0]
    piece = blocks // pieces
    more, count = plan_ref[MORE, 0], plan_ref[COUNT, 0]
    first = side_ref[0] * more
    copies = []
    for p in range(pieces):
        for block in range(p * piece, (p + 1) * piece):
            rank = plan_ref[RANK, block]
            place = jnp.where(rank < first, rank, rank - more)
            held = (rank < count) & ((rank < first) | (rank >= first + more))
            rows = own_ref[jnp.where(held, place, 0)]
            whole[block] = jnp.where(held, rows, jnp.zeros_like(rows))
        part = pl.ds(p * piece, piece)
        copies.append(pltpu.make_async_copy(whole.at[part], out_ref.at[part], sems.at[p]))
        copies[-1].start()
    for copy in copies:
        copy.wait()


def place_own(side, plan, own):
    blocks = plan.shape[1]
    shape = (blocks,) + own.shape[1:]
    smem = pl.BlockSpec(memory_space=pltpu.SMEM)
    return pl.pallas_call(
        place_own_kernel,
        out_shape=jax.ShapeDtypeStruct(shape, own.dtype),
        in_specs=[smem, smem, pl.BlockSpec(memory_space=pltpu.VMEM)],
        out_specs=pl.BlockSpec(memory_space=pltpu.HBM),
        scratch_shapes=[pltpu.VMEM(shape, own.dtype), pltpu.SemaphoreType.DMA((8,))],
        compiler_params=pltpu.CompilerParams(vmem_limit_bytes=8 * 2**20),
        cost_estimate=pl.CostEstimate(flops=0, bytes_accessed=4 * own.size, transcendentals=0),
    )(side, plan, own)


def place_others_kernel(side_ref, plan_ref, held_ref, *refs):
    parts, out_ref, sems = refs[:-2], refs[-2], refs[-1]
    position = side_ref[0] * sum(part.shape[0] for part in parts)
    for index, part in enumerate(parts):
        for q in range(part.shape[0]):
            target = out_ref.at[plan_ref[BLOCK, position + q]]
            pltpu.make_async_copy(part.at[q], target, sems.at[index]).start()
        position += part.shape[0]
    for index, part in enumerate(parts):
        pltpu.make_async_copy(part, part, sems.at[index]).wait()


def place_others(side, plan, held, parts):
    smem = pl.BlockSpec(memory_space=pltpu.SMEM)
    vmem = pl.BlockSpec(memory_space=pltpu.VMEM)
    hbm = pl.BlockSpec(memory_space=pltpu.HBM)
    size = sum(part.size for part in parts)
    return pl.pallas_call(
        place_others_kernel,
        out_shape=jax.ShapeDtypeStruct(held.shape, held.dtype),
        in_specs=[smem, smem, hbm] + [vmem] * len(parts),
        out_specs=hbm,
        scratch_shapes=[pltpu.SemaphoreType.DMA((len(parts),))],
        input_output_aliases={2: 0},
        compiler_params=pltpu.CompilerParams(vmem_limit_bytes=6 * 2**20),
        cost_estimate=pl.CostEstimate(flops=0, bytes_accessed=4 * size, transcendentals=0),
    )(side, plan, held, *parts)


def exchange(handed, side, plan, own):
    planes, cores = lax.axis_size("x"), lax.axis_size("c")
    steps = ((1, 1), (-1, -1)) if handed[1] else ((1, -1), (0, 0))
    start, parts = 0, []
    for size, step in zip(handed, steps):
        if size:
            pairs = [
                (core * planes + x, core * planes + (x + step[core]) % planes)
                for core in range(cores)
                for x in range(planes)
            ]
            parts.append(lax.ppermute(own[start : start + size], ("c", "x"), pairs))
            start += size
    held = place_own(side, plan, own)
    return place_others(side, plan, held, parts) if parts else held


def body(grads, owners, counts):
    blocks, rows_dev, width = grads.shape
    chips = lax.axis_size("yz")
    side = jnp.stack([lax.axis_index("x") % 2, lax.axis_index("yz")]).astype(jnp.int32)

    outgoing, plan, tier = make_plan(side, owners, counts, grads, chips)
    mine = lax.all_to_all(outgoing, "yz", split_axis=0, concat_axis=0, tiled=True)
    mine = mine.reshape(chips * rows_dev, width)
    theirs = lax.ppermute(mine, "c", [(0, 1), (1, 0)])
    tier = lax.clamp(0, tier[0], len(HANDED) - 1)
    done = refresh(side, plan, tier.reshape(1), mine, theirs, *gram(mine))
    own = lax.all_to_all(
        done.reshape(chips, rows_dev, width), "yz", split_axis=0, concat_axis=0, tiled=True
    )
    branches = [functools.partial(exchange, handed) for handed in HANDED]
    return lax.switch(tier, branches, side, plan, own)


def solution(mesh):
    fine = Mesh(mesh.devices.reshape(64, 2, 4), ("yz", "c", "x"))
    rows = P(None, ("yz", "c"), None)
    return jax.shard_map(body, mesh=fine, in_specs=(rows, P(), P()), out_specs=rows, check_vma=False)
```

```python
import functools

import jax
import jax.numpy as jnp
from jax import lax
from jax.experimental import pallas as pl
from jax.experimental.pallas import tpu as pltpu
from jax.sharding import Mesh
from jax.sharding import PartitionSpec as P

EPS = 1e-06
TILE = 256
HANDED = (
    *((size, 0) for size in (0, 4, 8, 10, 12, 14, 16, 18, 20)),
    *((16, 6), (17, 7), (19, 9), (21, 11), (25, 15), (29, 19), (37, 27)),
)
BLOCK, RANK, TIER, MORE, COUNT = range(5)


def down_columns(row):
    n = row.shape[1]
    return jnp.broadcast_to(row, (n, n)).T


def plan_kernel(
    side_ref, owners_ref, counts_ref, grads_ref, out_ref, plan_ref, tier_ref, whole, rows_ref, plan_sem, whole_sems
):
    piece = whole.shape[0] // whole_sems.shape[0]
    loads = []
    for p in range(whole_sems.shape[0]):
        part = pl.ds(p * piece, piece)
        loads.append(pltpu.make_async_copy(grads_ref.at[part], whole.at[part], whole_sems.at[p]))
        loads[-1].start()
    places, blocks = out_ref.shape[0], owners_ref.shape[1]
    square = (blocks, blocks)
    i = lax.broadcasted_iota(jnp.int32, square, 0)
    j = lax.broadcasted_iota(jnp.int32, square, 1)
    owners = jnp.broadcast_to(owners_ref[...], square)
    same = (down_columns(owners_ref[...]) == owners) & (i < j)
    slot = jnp.sum(jnp.where(same, 1, 0), axis=0, keepdims=True)
    have = jnp.sum(jnp.where(owners == i, down_columns(counts_ref[...]), 0), axis=0, keepdims=True)
    valid = jnp.where(slot < have, 1, 0)
    before = jnp.sum(jnp.where(i < j, down_columns(valid), 0), axis=0, keepdims=True)
    count = jnp.broadcast_to(jnp.sum(valid, axis=1, keepdims=True), (1, blocks))
    rank = jnp.where(slot < have, before, count + j[:1, :] - before)
    block = jnp.sum(jnp.where(down_columns(rank) == j, i, 0), axis=0, keepdims=True)
    tier, more = jnp.zeros_like(count), jnp.zeros_like(count)
    for smaller, larger in zip(HANDED, HANDED[1:]):
        above = count > places + sum(smaller)
        tier = jnp.where(above, tier + 1, tier)
        more = jnp.where(above, sum(larger), more)
    for index, row in ((BLOCK, block), (RANK, rank), (TIER, tier), (MORE, more), (COUNT, count)):
        rows_ref[index : index + 1, :] = row
    to_scalars = pltpu.make_async_copy(rows_ref, plan_ref, plan_sem)
    to_scalars.start()
    to_scalars.wait()
    for load in loads:
        load.wait()
    tier_ref[0] = plan_ref[TIER, 0]
    more = plan_ref[MORE, 0]
    first = side_ref[0] * more
    for place in range(places):
        position = jnp.where(place < first, place, place + more)
        out_ref[place] = whole[plan_ref[BLOCK, position]]


def make_plan(side, owners, counts, grads, places):
    blocks = grads.shape[0]
    vmem = pl.BlockSpec(memory_space=pltpu.VMEM)
    smem = pl.BlockSpec(memory_space=pltpu.SMEM)
    return pl.pallas_call(
        plan_kernel,
        out_shape=(
            pltpu.VMEM((places,) + grads.shape[1:], grads.dtype),
            jax.ShapeDtypeStruct((8, blocks), jnp.int32),
            jax.ShapeDtypeStruct((1,), jnp.int32),
        ),
        in_specs=[smem, vmem, vmem, pl.BlockSpec(memory_space=pltpu.HBM)],
        out_specs=(vmem, smem, smem),
        scratch_shapes=[
            pltpu.VMEM(grads.shape, grads.dtype),
            pltpu.VMEM((8, blocks), jnp.int32),
            pltpu.SemaphoreType.DMA,
            pltpu.SemaphoreType.DMA((8,)),
        ],
        compiler_params=pltpu.CompilerParams(vmem_limit_bytes=8 * 2**20),
    )(
        side,
        *(
            pltpu.with_memory_space_constraint(array, pltpu.HBM)
            for array in (owners.reshape(1, -1), counts.reshape(1, -1), grads)
        ),
    )


def first_dims(a, b):
    return lax.dot_general(a, b, (((0,), (0,)), ((), ())), preferred_element_type=jnp.float32)


def folded_squares(tile):
    squares = tile * tile
    folded = jnp.sum(squares.reshape(tile.shape[0] // 8, 8, tile.shape[1]), axis=0)
    return sum(folded[:, c : c + 128] for c in range(0, tile.shape[1], 128))


def gram_kernel(rows_ref, out_ref, squares_ref):
    width = rows_ref.shape[1]
    for j in range(0, width, TILE):
        out_ref[j:, j : j + TILE] = first_dims(rows_ref[:, j:], rows_ref[:, j : j + TILE])
    squares_ref[...] = folded_squares(rows_ref[...].astype(jnp.float32))


def gram(rows):
    count, width = rows.shape
    vmem = pl.BlockSpec(memory_space=pltpu.VMEM)
    return pl.pallas_call(
        gram_kernel,
        out_shape=(
            jax.ShapeDtypeStruct((width, width), jnp.float32),
            jax.ShapeDtypeStruct((8, 128), jnp.float32),
        ),
        in_specs=[vmem],
        out_specs=(vmem, vmem),
        compiler_params=pltpu.CompilerParams(vmem_limit_bytes=12 * 2**20),
        cost_estimate=pl.CostEstimate(
            flops=2 * count * width**2, bytes_accessed=2 * count * width + 4 * width**2, transcendentals=0
        ),
    )(rows)


def on_diagonal(tile):
    r = lax.broadcasted_iota(jnp.int32, tile.shape, 0)
    c = lax.broadcasted_iota(jnp.int32, tile.shape, 1)
    return r == c


def refresh_kernel(side_ref, plan_ref, tier_ref, mine_ref, theirs_ref, gram_ref, squares_ref, out_ref, *scratch):
    del tier_ref
    root, square, rest, product, turned = scratch
    rows, width = mine_ref.shape
    place, more = side_ref[1], plan_ref[MORE, 0]
    position = jnp.where(place < side_ref[0] * more, place, place + more)
    valid = jnp.where(position < plan_ref[COUNT, 0], 1.0, 0.0)

    total_sq = squares_ref[...] + folded_squares(theirs_ref[...].astype(jnp.float32))
    total_sq = jnp.sum(total_sq, keepdims=True)
    scale_c = total_sq / width + EPS
    quarter = lax.rsqrt(jnp.sqrt(scale_c)) * 0.25
    slope = quarter / scale_c
    diag = 5.0 * quarter - EPS * slope

    turned[...] = theirs_ref[...].T
    for j in range(0, width, TILE):
        cols = slice(j, j + TILE)
        tile = gram_ref[j:, cols] + jnp.dot(turned[j:, :], theirs_ref[:, cols], preferred_element_type=jnp.float32)
        tile = -slope * tile
        top = tile[:TILE]
        top = jnp.where(on_diagonal(top), diag + top, top)
        kept = top.astype(jnp.bfloat16)
        root[cols, cols] = kept
        kept = kept.astype(jnp.float32)
        off = jnp.where(on_diagonal(top), 2.0 * (top - kept) * kept, 0.0)
        rest[:, cols] = jnp.sum(off, axis=0, keepdims=True)
        if j + TILE < width:
            below = tile[TILE:].astype(jnp.bfloat16)
            root[j + TILE :, cols] = below
            root[cols, j + TILE :] = below.T

    for j in range(0, width, TILE):
        cols = slice(j, j + TILE)
        tile = jnp.dot(root[j:, :], root[:, cols], preferred_element_type=jnp.float32)
        top = tile[:TILE]
        kept = top.astype(jnp.bfloat16)
        square[cols, cols] = kept
        off = jnp.where(on_diagonal(top), top - kept.astype(jnp.float32), 0.0)
        rest[:, cols] += jnp.sum(off, axis=0, keepdims=True)
        if j + TILE < width:
            below = tile[TILE:].astype(jnp.bfloat16)
            square[j + TILE :, cols] = below
            square[cols, j + TILE :] = below.T

    squares = jnp.zeros((8, 128), jnp.float32)
    for j in range(0, width, TILE):
        cols = slice(j, j + TILE)
        for ref in (mine_ref, theirs_ref):
            done = jnp.dot(ref[...], square[:, cols], preferred_element_type=jnp.float32)
            done = done + ref[:, cols].astype(jnp.float32) * rest[:, cols]
            squares += folded_squares(done)
            if ref is mine_ref:
                product[:, cols] = done
    product_sq = jnp.sum(squares, keepdims=True)
    graft = jnp.sqrt((total_sq + EPS) / (product_sq + EPS)) * valid
    out_ref[...] = (product[...] * graft).astype(jnp.bfloat16)


def refresh(side, plan, tier, mine, theirs, mine_gram, mine_squares):
    rows, width = mine.shape
    vmem = pl.BlockSpec(memory_space=pltpu.VMEM)
    smem = pl.BlockSpec(memory_space=pltpu.SMEM)
    return pl.pallas_call(
        refresh_kernel,
        out_shape=jax.ShapeDtypeStruct((rows, width), jnp.bfloat16),
        in_specs=[smem, smem, smem, vmem, vmem, vmem, vmem],
        out_specs=vmem,
        scratch_shapes=[
            pltpu.VMEM((width, width), jnp.bfloat16),
            pltpu.VMEM((width, width), jnp.bfloat16),
            pltpu.VMEM((1, width), jnp.float32),
            pltpu.VMEM((rows, width), jnp.float32),
            pltpu.VMEM((width, rows), jnp.bfloat16),
        ],
        compiler_params=pltpu.CompilerParams(vmem_limit_bytes=14 * 2**20),
        cost_estimate=pl.CostEstimate(flops=4 * width**3, bytes_accessed=6 * rows * width, transcendentals=0),
    )(side, plan, tier, mine, theirs, mine_gram, mine_squares)


def place_own_kernel(side_ref, plan_ref, own_ref, out_ref, whole, sems):
    blocks = out_ref.shape[0]
    pieces = sems.shape[0]
    piece = blocks // pieces
    more, count = plan_ref[MORE, 0], plan_ref[COUNT, 0]
    first = side_ref[0] * more
    copies = []
    for p in range(pieces):
        for block in range(p * piece, (p + 1) * piece):
            rank = plan_ref[RANK, block]
            place = jnp.where(rank < first, rank, rank - more)
            held = (rank < count) & ((rank < first) | (rank >= first + more))
            rows = own_ref[jnp.where(held, place, 0)]
            whole[block] = jnp.where(held, rows, jnp.zeros_like(rows))
        part = pl.ds(p * piece, piece)
        copies.append(pltpu.make_async_copy(whole.at[part], out_ref.at[part], sems.at[p]))
        copies[-1].start()
    for copy in copies:
        copy.wait()


def place_own(side, plan, own):
    blocks = plan.shape[1]
    shape = (blocks,) + own.shape[1:]
    smem = pl.BlockSpec(memory_space=pltpu.SMEM)
    return pl.pallas_call(
        place_own_kernel,
        out_shape=jax.ShapeDtypeStruct(shape, own.dtype),
        in_specs=[smem, smem, pl.BlockSpec(memory_space=pltpu.VMEM)],
        out_specs=pl.BlockSpec(memory_space=pltpu.HBM),
        scratch_shapes=[pltpu.VMEM(shape, own.dtype), pltpu.SemaphoreType.DMA((8,))],
        compiler_params=pltpu.CompilerParams(vmem_limit_bytes=8 * 2**20),
        cost_estimate=pl.CostEstimate(flops=0, bytes_accessed=4 * own.size, transcendentals=0),
    )(side, plan, own)


def place_others_kernel(side_ref, plan_ref, held_ref, *refs):
    parts, out_ref, sems = refs[:-2], refs[-2], refs[-1]
    position = side_ref[0] * sum(part.shape[0] for part in parts)
    for index, part in enumerate(parts):
        for q in range(part.shape[0]):
            target = out_ref.at[plan_ref[BLOCK, position + q]]
            pltpu.make_async_copy(part.at[q], target, sems.at[index]).start()
        position += part.shape[0]
    for index, part in enumerate(parts):
        pltpu.make_async_copy(part, part, sems.at[index]).wait()


def place_others(side, plan, held, parts):
    smem = pl.BlockSpec(memory_space=pltpu.SMEM)
    vmem = pl.BlockSpec(memory_space=pltpu.VMEM)
    hbm = pl.BlockSpec(memory_space=pltpu.HBM)
    size = sum(part.size for part in parts)
    return pl.pallas_call(
        place_others_kernel,
        out_shape=jax.ShapeDtypeStruct(held.shape, held.dtype),
        in_specs=[smem, smem, hbm] + [vmem] * len(parts),
        out_specs=hbm,
        scratch_shapes=[pltpu.SemaphoreType.DMA((len(parts),))],
        input_output_aliases={2: 0},
        compiler_params=pltpu.CompilerParams(vmem_limit_bytes=6 * 2**20),
        cost_estimate=pl.CostEstimate(flops=0, bytes_accessed=4 * size, transcendentals=0),
    )(side, plan, held, *parts)


def exchange(handed, side, plan, own):
    planes, cores = lax.axis_size("x"), lax.axis_size("c")
    steps = ((1, 1), (-1, -1)) if handed[1] else ((1, -1), (0, 0))
    start, parts = 0, []
    for size, step in zip(handed, steps):
        if size:
            pairs = [
                (core * planes + x, core * planes + (x + step[core]) % planes)
                for core in range(cores)
                for x in range(planes)
            ]
            parts.append(lax.ppermute(own[start : start + size], ("c", "x"), pairs))
            start += size
    held = place_own(side, plan, own)
    return place_others(side, plan, held, parts) if parts else held


def body(grads, owners, counts):
    blocks, rows_dev, width = grads.shape
    chips = lax.axis_size("yz")
    side = jnp.stack([lax.axis_index("x") % 2, lax.axis_index("yz")]).astype(jnp.int32)

    outgoing, plan, tier = make_plan(side, owners, counts, grads, chips)
    mine = lax.all_to_all(outgoing, "yz", split_axis=0, concat_axis=0, tiled=True)
    mine = mine.reshape(chips * rows_dev, width)
    theirs = lax.ppermute(mine, "c", [(0, 1), (1, 0)])
    tier = lax.clamp(0, tier[0], len(HANDED) - 1)
    done = refresh(side, plan, tier.reshape(1), mine, theirs, *gram(mine))
    own = lax.all_to_all(
        done.reshape(chips, rows_dev, width), "yz", split_axis=0, concat_axis=0, tiled=True
    )
    branches = [functools.partial(exchange, handed) for handed in HANDED]
    return lax.switch(tier, branches, side, plan, own)


def solution(mesh):
    fine = Mesh(mesh.devices.reshape(64, 2, 4), ("yz", "c", "x"))
    rows = P(None, ("yz", "c"), None)
    return jax.shard_map(body, mesh=fine, in_specs=(rows, P(), P()), out_specs=rows, check_vma=False)
```
